1024 devices in a mesh: dp: 128 (over z_lo, y, core), tensor: 8 (over z_hi, x).
Axes of the slice: x: 4, y: 4, z: 32 (z_hi: 2, z_lo: 16; z = z_hi * 16 + z_lo), core: 2. Of those that a mesh axis runs over, the one named last changes fastest.
Arguments:
- grads: bfloat16 [128, 4096, 1024], P('dp', None, 'tensor'), may hold values from -16 to 16
- errors: bfloat16 [128, 4096, 1024], P('dp', None, 'tensor'), may hold values from -3 to 3
- basis: float32 [1024, 64], P('tensor'), may hold values from -6 to 6
Outputs:
- approx: bfloat16 [4096, 1024], P(None, 'tensor')
- new_errors: bfloat16 [128, 4096, 1024], P('dp', None, 'tensor')
- new_basis: float32 [1024, 64], P('tensor')
The draws below stay inside these ranges and needn't reach their ends.
All inputs are finite; a program needn't handle non-finite values.
Results may differ from the reference program's by a relative error of at most 0.009.
Values may be sent and summed in bfloat16 or wider, within the bound.
A program may use at most 32 MiB of HBM per device.

```python
import jax
import jax.numpy as jnp
from jax import lax

COLS = 1024
ROWS = 4096
RANK = 64
REPLICAS = 128


def draw_grads(key, part):
    key = jax.random.fold_in(key, 11)
    shared_key, own_key = jax.random.split(key, 2)
    shared = jax.random.normal(shared_key, (ROWS, COLS), jnp.float32)
    own = jax.random.normal(own_key, (REPLICAS, ROWS, COLS), jnp.float32)
    steps = jnp.arange(REPLICAS, dtype=jnp.float32) / max(REPLICAS - 1, 1)
    replica_scale = jnp.exp(steps * 1.0986)[:, None, None]
    values = 0.4 * shared[None] + 1.5 * replica_scale * own
    return jnp.clip(values, -16.0, 16.0).astype(jnp.bfloat16)


def steps_of(key, extent, pieces, smallest, high):
    level = 1.0
    for axis_at, blocks in pieces:
        draws = jax.random.uniform(jax.random.fold_in(jax.random.fold_in(key, 6), axis_at), (blocks,), jnp.float32, smallest / len(pieces), high / len(pieces))
        level = level * jnp.repeat(jnp.exp(draws), extent[axis_at] // blocks).reshape((-1,) + (1,) * (len(extent) - 1 - axis_at))
    return level


def scatter_about(stream_key, dims, spread, limit, cuts=(), kind=jnp.bfloat16):
    values = jax.random.normal(stream_key, dims, jnp.float32) * spread
    if len(cuts) > 0:
        values = steps_of(stream_key, dims, cuts, -0.22, 0.18) * values
    return jnp.clip(values, min=-limit, max=limit).astype(kind)


def setup_inputs(seed: int = 0) -> dict:
    arg_keys = jax.random.split(jax.random.key(seed), 4)
    return {
        "grads": draw_grads(jax.random.fold_in(arg_keys[3], 71), 0),
        "errors": scatter_about(arg_keys[1], (REPLICAS, ROWS, COLS), 0.5, 3.0, ((0, 128), (2, 8))),
        "basis": scatter_about(arg_keys[2], (COLS, RANK), 1.0, 6.0, ((0, 8),), jnp.float32),
    }


def combine_one(grads, errors, replica):
    grad_row = lax.dynamic_index_in_dim(grads, replica, 0, keepdims=False)
    error_row = lax.dynamic_index_in_dim(errors, replica, 0, keepdims=False)
    return (grad_row.astype(jnp.float32) + error_row.astype(jnp.float32)).astype(jnp.bfloat16)

def reference(grads, errors, basis):
    replicas = grads.shape[0]
    indices = jnp.arange(replicas, dtype=jnp.int32)
    basis_bf = basis.astype(jnp.bfloat16)

    def add_left(running, replica):
        combined = combine_one(grads, errors, replica)
        return (running + jnp.dot(combined.astype(jnp.float32), basis_bf.astype(jnp.float32), preferred_element_type=jnp.float32), None)
    left_factor, _ = lax.scan(add_left, jnp.zeros((ROWS, RANK), jnp.float32), indices)
    left_factor = left_factor / replicas
    gram_matrix = jnp.dot(left_factor.T, left_factor, precision=lax.Precision.HIGHEST)
    lower_factor = jnp.linalg.cholesky(gram_matrix)
    orthonormal = lax.linalg.triangular_solve(lower_factor, left_factor, left_side=False, lower=True, transpose_a=True).astype(jnp.bfloat16)

    def add_right(running, replica):
        combined = combine_one(grads, errors, replica)
        return (running + lax.dot_general(combined.astype(jnp.float32), orthonormal.astype(jnp.float32), (((0,), (0,)), ((), ())), preferred_element_type=jnp.float32), None)
    new_basis, _ = lax.scan(add_right, jnp.zeros((COLS, RANK), jnp.float32), indices)
    new_basis = new_basis / replicas
    basis_new_bf = new_basis.astype(jnp.bfloat16)
    full_approx = lax.dot_general(orthonormal.astype(jnp.float32), basis_new_bf.astype(jnp.float32), (((1,), (1,)), ((), ())), preferred_element_type=jnp.float32)

    def error_one(replica):
        combined = combine_one(grads, errors, replica)
        return (combined.astype(jnp.float32) - full_approx).astype(jnp.bfloat16)
    new_errors = lax.map(error_one, indices)
    return (full_approx.astype(jnp.bfloat16), new_errors, new_basis)
```

```python
import functools

import jax
import jax.numpy as jnp
from jax import lax
from jax.experimental import pallas as pl
from jax.experimental.pallas import tpu as pltpu
from jax.sharding import PartitionSpec as P

MESH = pl.DeviceIdType.MESH
F32, BF16 = jnp.float32, jnp.bfloat16
COLS, RANK = 128, 64
HALF = 2048
OWN = 1024
BLOCK = 64
PART = 16
CHUNK = 256


def device(x, y, z, core):
    return ((z & 15) * 8 + y * 2 + core, (z >> 4) * 4 + x)


def rows(start, size):
    return pl.ds(pl.multiple_of(start, size), size)


def send(src, dst, send_sem, recv_sem, to):
    copy = pltpu.make_async_remote_copy(
        src_ref=src, dst_ref=dst, send_sem=send_sem, recv_sem=recv_sem, device_id=to, device_id_type=MESH
    )
    copy.start()


def wait(ref, sem):
    pltpu.make_async_copy(ref, ref, sem).wait()


def split(value):
    high = value.astype(BF16)
    low = (value - high.astype(F32)).astype(BF16)
    return high, low


def twice(value):
    zeros = jnp.zeros_like(value)
    return jnp.concatenate(
        [jnp.concatenate([value, zeros], axis=1), jnp.concatenate([zeros, value], axis=1)], axis=0
    )


def inverse_factor(gram):
    tiles = RANK // 8
    rows_at = lax.broadcasted_iota(jnp.int32, (8, 128), 0)
    m = [gram[8 * b : 8 * b + 8, :] for b in range(tiles)]
    pivots = []
    for k in range(RANK):
        at, sub = divmod(k, 8)
        pivot_row = m[at][sub : sub + 1, :]
        pivot = pivot_row[:, k : k + 1]
        pivots.append(pivot)
        scaled = pivot_row * (1.0 / pivot)
        for b in range(at, tiles):
            update = m[b][:, k : k + 1] * scaled
            if b == at:
                update = jnp.where(rows_at > sub, update, 0.0)
            m[b] = m[b] - update
    out = []
    for b in range(tiles):
        scale = jnp.concatenate(pivots[8 * b : 8 * b + 8], axis=0)
        out.append(m[b] * lax.rsqrt(scale))
    return jnp.concatenate(out, axis=0)


def exchange_kernel(
    replicas, grads, errors, basis, q_out, comb_out, right_out,
    g_in, e_in, comb, blocks, part, from_core, plane_in, plane_sum, near_in, near_sum, far_in, full, pieces, grams, q,
    right, right_core, right_y, right_near, right_near_sum, right_far, right_full,
    local_sem, core_send, core_recv, send_sem, recv_sem, far_send, far_recv,
):
    d, t = lax.axis_index("dp"), lax.axis_index("tensor")
    core, y, z, x = d & 1, (d >> 1) & 3, (t >> 2) * 16 + (d >> 3), t & 3
    near, far, mine = z & 3, z >> 2, y * 4 + x
    other = device(x, y, z, 1 - core)
    own, theirs = core * OWN, (1 - core) * OWN

    def plane(i, j):
        return (x + j) & 3, (y + i) & 3

    def near_at(o):
        return (near + o) & 3

    def near_device(o):
        return device(x, y, (z & 28) | near_at(o), core)

    def in_line(o):
        return device(x, y, (z & 19) | (((far + o) & 3) << 2), core)

    up, down = device(x, y, (z + 4) & 31, core), device(x, y, (z + 28) & 31, core)
    offsets = [(i, j) for i in range(4) for j in range(4) if (i, j) != (0, 0)]

    for n, start in enumerate((theirs, own)):
        for base in (0, HALF):
            here = rows(base + start, OWN)
            pltpu.make_async_copy(grads.at[0, here], g_in.at[here], local_sem.at[n]).start()
            pltpu.make_async_copy(errors.at[0, here], e_in.at[here], local_sem.at[n]).start()

    barrier = pltpu.get_barrier_semaphore()
    partners = [other, up, down] + [near_device(o) for o in (1, 2, 3)]
    partners += [device(*plane(i, j), z, core) for i, j in offsets]
    for to in partners:
        pl.semaphore_signal(barrier, inc=1, device_id=to, device_id_type=MESH)

    blocks[...] = twice(basis[...].astype(BF16))
    lanes = lax.broadcasted_iota(jnp.int32, (RANK, 128), 1)
    at = lax.broadcasted_iota(jnp.int32, (RANK, 128), 0)

    def product(start):
        both = []
        for base in (0, HALF):
            here = rows(base + start, CHUNK)
            both.append((g_in[here, :].astype(F32) + e_in[here, :].astype(F32)).astype(BF16))
        value = jnp.concatenate(both, axis=1)
        comb[rows(start, CHUNK), :] = value
        part[rows(start, CHUNK), :] = lax.dot_general(
            value, blocks[...], (((1,), (1,)), ((), ())), preferred_element_type=F32
        )

    order = [((y + i) & 3) * CHUNK for i in range(4)]
    wait(g_in, local_sem.at[0])
    for i in range(4):
        product(theirs + order[i])
    pl.semaphore_wait(barrier, len(partners))
    for i in range(4):
        send(part.at[rows(theirs + order[i], CHUNK)], from_core.at[i], core_send.at[i], core_recv.at[i], other)
    wait(g_in, local_sem.at[1])
    for i in range(4):
        product(own + order[i])
    for i in range(4):
        wait(from_core.at[i], core_recv.at[i])
        here = rows(own + order[i], CHUNK)
        part[here, :] = part[here, :] + from_core[i]
        for j in range(4):
            if (i, j) != (0, 0):
                px, py = plane(i, j)
                src = part.at[rows(own + (py * 4 + px) * BLOCK, BLOCK)]
                send(src, plane_in.at[mine], send_sem.at[0], recv_sem.at[0], device(px, py, z, core))
    comb_copy = pltpu.make_async_copy(comb, comb_out, local_sem.at[2])
    comb_copy.start()
    plane_in[mine] = part[rows(own + mine * BLOCK, BLOCK), :]
    wait(plane_in.at[0:15], recv_sem.at[0])
    total = plane_in[0]
    for n in range(1, 16):
        total = total + plane_in[n]
    plane_sum[...] = total

    for o in (2, 1, 3):
        send(plane_sum.at[rows(near_at(o) * PART, PART)], near_in.at[near], send_sem.at[1], recv_sem.at[1], near_device(o))
    near_in[near] = plane_sum[rows(near * PART, PART), :]
    wait(near_in.at[0:3], recv_sem.at[1])
    near_sum[...] = ((near_in[0] + near_in[1]) + near_in[2]) + near_in[3]

    far_in[far] = near_sum[...]
    for step in range(4):
        slot = (far - step) & 7
        src = near_sum if step == 0 else far_in.at[slot]
        send(src, far_in.at[slot], far_send.at[0, step], far_recv.at[0, step], up)
        if step < 3:
            slot = (far + step) & 7
            src = near_sum if step == 0 else far_in.at[slot]
            send(src, far_in.at[slot], far_send.at[1, step], far_recv.at[1, step], down)
        wait(near_sum, far_recv.at[0, step])
        if step < 3:
            wait(near_sum, far_recv.at[1, step])
    total = far_in[0]
    for n in range(1, 8):
        total = total + far_in[n]
    block = own + mine * BLOCK
    piece = full.at[rows(block + near * PART, PART)]
    piece[...] = total * (1.0 / replicas)

    for o in (2, 1, 3):
        send(piece, piece, send_sem.at[2], recv_sem.at[2], near_device(o))
    wait(full.at[0 : 3 * PART], recv_sem.at[2])
    piece = full.at[rows(block, BLOCK)]
    for i, j in offsets:
        send(piece, piece, send_sem.at[3], recv_sem.at[3], device(*plane(i, j), z, core))
    wait(full.at[0 : 15 * BLOCK], recv_sem.at[3])
    piece = full.at[rows(own, OWN)]
    send(piece, piece, core_send.at[4], core_recv.at[4], other)

    def gram_of(start):
        total = None
        for i in range(4):
            here = rows(start + i * CHUNK, CHUNK)
            value = jnp.concatenate(split(full[here, :]), axis=1)
            pieces[here, :] = value
            term = lax.dot_general(value, value, (((0,), (0,)), ((), ())), preferred_element_type=F32)
            total = term if total is None else total + term
        return total

    grams[core] = gram_of(own)
    wait(piece, core_recv.at[4])
    grams[1 - core] = gram_of(theirs)
    gram = grams[0] + grams[1]
    gram = (gram[0:128, 0:128] + gram[128:256, 128:256]) + (gram[0:128, 128:256] + gram[128:256, 0:128])
    gram = gram[0:RANK, :] + pltpu.roll(gram[RANK:128, :], RANK, 1)
    factor = inverse_factor(jnp.where(lanes < RANK, gram, jnp.where(lanes == at + RANK, 1.0, 0.0)))
    inverse = jnp.where(lanes < RANK, 0.0, factor)
    inverse = jnp.concatenate([pltpu.roll(inverse, RANK, 1), inverse], axis=0)
    high, low = split(inverse)
    weights = jnp.concatenate([jnp.concatenate([high, high], axis=1), jnp.concatenate([low, low], axis=1)], axis=0)

    right_sum = jnp.zeros((128, 2 * COLS), F32)
    for i in range(HALF // CHUNK):
        here = pl.ds(i * CHUNK, CHUNK)
        value = lax.dot_general(pieces[here, :], weights, (((1,), (1,)), ((), ())), preferred_element_type=F32)
        value = (value[:, 0:128] + value[:, 128:256]).astype(BF16)
        q[here, :] = value
        right_sum += lax.dot_general(value, comb[here, :], (((0,), (0,)), ((), ())), preferred_element_type=F32)
    right[...] = right_sum[0:RANK, 0:COLS] + right_sum[RANK:128, COLS : 2 * COLS]

    send(right.at[rows((1 - core) * 32, 32)], right_core, core_send.at[5], core_recv.at[5], other)
    q_copy = pltpu.make_async_copy(q, q_out, local_sem.at[3])
    q_copy.start()
    wait(right_core, core_recv.at[5])
    base = core * 32
    here = rows(base, 32)
    right[here, :] = right[here, :] + right_core[...]
    for i in (2, 1, 3):
        py = (y + i) & 3
        send(right.at[rows(base + py * 8, 8)], right_y.at[y], send_sem.at[4], recv_sem.at[4], device(x, py, z, core))
    right_y[y] = right[rows(base + y * 8, 8), :]
    wait(right_y.at[0:3], recv_sem.at[4])
    right_near_sum[0] = ((right_y[0] + right_y[1]) + right_y[2]) + right_y[3]
    right_near[near] = right_near_sum[0]
    for o in (2, 1, 3):
        send(right_near_sum.at[0], right_near.at[near], send_sem.at[5], recv_sem.at[5], near_device(o))
    wait(right_near.at[0:3], recv_sem.at[5])
    right_near_sum[1] = ((right_near[0] + right_near[1]) + right_near[2]) + right_near[3]
    line = far & 3
    right_far[line] = right_near_sum[1]
    for o in (2, 1, 3):
        send(right_near_sum.at[1], right_far.at[line], send_sem.at[6], recv_sem.at[6], in_line(o))
    wait(right_far.at[0:3], recv_sem.at[6])
    total = ((right_far[0] + right_far[1]) + right_far[2]) + right_far[3]
    piece = right_full.at[rows(base + y * 8, 8)]
    piece[...] = total * (1.0 / replicas)
    for i in (2, 1, 3):
        send(piece, piece, send_sem.at[7], recv_sem.at[7], device(x, (y + i) & 3, z, core))
    wait(right_full.at[0:24], recv_sem.at[7])
    piece = right_full.at[rows(base, 32)]
    send(piece, piece, core_send.at[6], core_recv.at[6], other)
    wait(piece, core_recv.at[6])
    right_out[...] = right_full[...]

    for i in range(4):
        wait(from_core.at[i], core_send.at[i])
    wait(full.at[0:OWN], core_send.at[4])
    wait(right_core, core_send.at[5])
    wait(right_core, core_send.at[6])
    wait(plane_in.at[0:15], send_sem.at[0])
    wait(near_in.at[0:3], send_sem.at[1])
    wait(near_in.at[0:3], send_sem.at[2])
    wait(full.at[0 : 15 * BLOCK], send_sem.at[3])
    for n in (4, 5, 6):
        wait(right_y.at[0:3], send_sem.at[n])
    wait(right_full.at[0:24], send_sem.at[7])
    for step in range(4):
        wait(near_sum, far_send.at[0, step])
        if step < 3:
            wait(near_sum, far_send.at[1, step])
    comb_copy.wait()
    q_copy.wait()


def finish_kernel(q, comb, right, approx, new_errors):
    full = jnp.dot(q[...], twice(right[...].astype(BF16)), preferred_element_type=F32)
    error = (comb[...].astype(F32) - full).astype(BF16)
    full = full.astype(BF16)
    for n in range(2):
        approx[n] = full[:, COLS * n : COLS * (n + 1)]
        new_errors[n] = error[:, COLS * n : COLS * (n + 1)]


def local(replicas, grads, errors, basis):
    vmem, dma = pltpu.VMEM, pltpu.SemaphoreType.DMA
    q, comb, right = pl.pallas_call(
        functools.partial(exchange_kernel, replicas),
        name="exchange",
        out_shape=(
            jax.ShapeDtypeStruct((HALF, 128), BF16),
            jax.ShapeDtypeStruct((HALF, 2 * COLS), BF16),
            jax.ShapeDtypeStruct((RANK, COLS), F32),
        ),
        in_specs=[pl.BlockSpec(memory_space=pl.ANY)] * 2 + [pl.BlockSpec(memory_space=vmem)],
        out_specs=(pl.BlockSpec(memory_space=pl.ANY),) * 2 + (pl.BlockSpec(memory_space=vmem),),
        scratch_shapes=[
            vmem((2 * HALF, COLS), BF16), vmem((2 * HALF, COLS), BF16), vmem((HALF, 2 * COLS), BF16),
            vmem((128, 2 * COLS), BF16), vmem((HALF, 128), F32), vmem((4, CHUNK, 128), F32),
            vmem((16, BLOCK, 128), F32), vmem((BLOCK, 128), F32), vmem((4, PART, 128), F32), vmem((PART, 128), F32),
            vmem((8, PART, 128), F32), vmem((HALF, 128), F32), vmem((HALF, 256), BF16), vmem((2, 256, 256), F32),
            vmem((HALF, 128), BF16),
            vmem((RANK, COLS), F32), vmem((32, COLS), F32), vmem((4, 8, COLS), F32), vmem((4, 8, COLS), F32),
            vmem((2, 8, COLS), F32), vmem((4, 8, COLS), F32), vmem((RANK, COLS), F32),
            dma((4,)), dma((7,)), dma((7,)), dma((8,)), dma((8,)), dma((2, 4)), dma((2, 4)),
        ],
        compiler_params=pltpu.CompilerParams(collective_id=0, has_side_effects=True, vmem_limit_bytes=56 << 20),
    )(grads, errors, basis.T)
    whole = pl.BlockSpec((RANK, COLS), lambda i: (0, 0))
    pair = pl.BlockSpec((2, 512, COLS), lambda i: (0, i, 0))
    approx, new_errors = pl.pallas_call(
        finish_kernel,
        name="finish",
        grid=(HALF // 512,),
        out_shape=(
            jax.ShapeDtypeStruct((2, HALF, COLS), BF16),
            jax.ShapeDtypeStruct((2, HALF, COLS), BF16),
        ),
        in_specs=[pl.BlockSpec((512, 128), lambda i: (i, 0)), pl.BlockSpec((512, 2 * COLS), lambda i: (i, 0)), whole],
        out_specs=(pair, pair),
    )(q, comb, right)
    return approx.reshape(2 * HALF, COLS), new_errors.reshape(1, 2 * HALF, COLS), right.T


def solution(mesh):
    placed = (P("dp", None, "tensor"), P("dp", None, "tensor"), P("tensor", None))
    return jax.shard_map(
        functools.partial(local, mesh.shape["dp"]),
        mesh=mesh,
        in_specs=placed,
        out_specs=(P(None, "tensor"), P("dp", None, "tensor"), P("tensor", None)),
        check_vma=False,
    )
```

```python
import functools

import jax
import jax.numpy as jnp
from jax import lax
from jax.experimental import pallas as pl
from jax.experimental.pallas import tpu as pltpu
from jax.sharding import PartitionSpec as P

MESH = pl.DeviceIdType.MESH
F32, BF16 = jnp.float32, jnp.bfloat16
COLS, RANK = 128, 64
HALF = 2048
OWN = 1024
BLOCK = 64
PART = 16
CHUNK = 256


def device(x, y, z, core):
    return ((z & 15) * 8 + y * 2 + core, (z >> 4) * 4 + x)


def rows(start, size):
    return pl.ds(pl.multiple_of(start, size), size)


def send(src, dst, send_sem, recv_sem, to):
    copy = pltpu.make_async_remote_copy(
        src_ref=src, dst_ref=dst, send_sem=send_sem, recv_sem=recv_sem, device_id=to, device_id_type=MESH
    )
    copy.start()


def wait(ref, sem):
    pltpu.make_async_copy(ref, ref, sem).wait()


def split(value):
    high = value.astype(BF16)
    low = (value - high.astype(F32)).astype(BF16)
    return high, low


def twice(value):
    zeros = jnp.zeros_like(value)
    return jnp.concatenate(
        [jnp.concatenate([value, zeros], axis=1), jnp.concatenate([zeros, value], axis=1)], axis=0
    )


def inverse_factor(gram):
    tiles = RANK // 8
    rows_at = lax.broadcasted_iota(jnp.int32, (8, 128), 0)
    m = [gram[8 * b : 8 * b + 8, :] for b in range(tiles)]
    pivots = []
    for k in range(RANK):
        at, sub = divmod(k, 8)
        pivot_row = m[at][sub : sub + 1, :]
        pivot = pivot_row[:, k : k + 1]
        pivots.append(pivot)
        scaled = pivot_row * (1.0 / pivot)
        for b in range(at, tiles):
            update = m[b][:, k : k + 1] * scaled
            if b == at:
                update = jnp.where(rows_at > sub, update, 0.0)
            m[b] = m[b] - update
    out = []
    for b in range(tiles):
        scale = jnp.concatenate(pivots[8 * b : 8 * b + 8], axis=0)
        out.append(m[b] * lax.rsqrt(scale))
    return jnp.concatenate(out, axis=0)


def exchange_kernel(
    replicas, grads, errors, basis, q_out, comb_out, right_out,
    g_in, e_in, comb, blocks, part, from_core, plane_in, plane_sum, near_in, near_sum, far_in, full, mates, pieces, grams,
    q, right, right_in, right_near, right_near_sum, right_far, right_full,
    local_sem, core_send, core_recv, send_sem, recv_sem, far_send, far_recv,
):
    d, t = lax.axis_index("dp"), lax.axis_index("tensor")
    core, y, z, x = d & 1, (d >> 1) & 3, (t >> 2) * 16 + (d >> 3), t & 3
    near, far, mine = z & 3, z >> 2, y * 4 + x
    other = device(x, y, z, 1 - core)
    own, theirs = core * OWN, (1 - core) * OWN

    def plane(i, j):
        return (x + j) & 3, (y + i) & 3

    def near_at(o):
        return (near + o) & 3

    def near_device(o, j=0):
        return device((x + j) & 3, y, (z & 28) | near_at(o), core)

    def in_line(o):
        return device(x, y, (z & 19) | (((far + o) & 3) << 2), core)

    def in_ring(o):
        return device(x, y, (z + 4 * o) & 31, core)

    def mate(c, i):
        to_core, to_y = core ^ c, (y + i) & 3
        return to_core * 4 + to_y, device(x, to_y, z, to_core)

    offsets = [(i, j) for i in range(4) for j in range(4) if (i, j) != (0, 0)]
    mate_offsets = [(0, 2), (1, 2), (0, 1), (0, 3), (1, 1), (1, 3), (1, 0)]
    ring_offsets = [2, -2, 1, -1]

    for n, start in enumerate((theirs, own)):
        for base in (0, HALF):
            here = rows(base + start, OWN)
            pltpu.make_async_copy(grads.at[0, here], g_in.at[here], local_sem.at[n]).start()
            pltpu.make_async_copy(errors.at[0, here], e_in.at[here], local_sem.at[n]).start()

    barrier = pltpu.get_barrier_semaphore()
    partners = [in_ring(o) for o in ring_offsets] + [near_device(o) for o in (1, 2, 3)]
    partners += [device(*plane(i, j), z, core) for i, j in offsets] + [other]
    for to in partners:
        pl.semaphore_signal(barrier, inc=1, device_id=to, device_id_type=MESH)

    blocks[...] = twice(basis[...].astype(BF16))
    lanes = lax.broadcasted_iota(jnp.int32, (RANK, 128), 1)
    at = lax.broadcasted_iota(jnp.int32, (RANK, 128), 0)

    def product(start):
        both = []
        for base in (0, HALF):
            here = rows(base + start, CHUNK)
            both.append((g_in[here, :].astype(F32) + e_in[here, :].astype(F32)).astype(BF16))
        value = jnp.concatenate(both, axis=1)
        comb[rows(start, CHUNK), :] = value
        part[rows(start, CHUNK), :] = lax.dot_general(
            value, blocks[...], (((1,), (1,)), ((), ())), preferred_element_type=F32
        )

    order = [((y + i) & 3) * CHUNK for i in range(4)]
    wait(g_in, local_sem.at[0])
    for i in range(4):
        product(theirs + order[i])
    pl.semaphore_wait(barrier, len(partners))
    for i in range(4):
        send(part.at[rows(theirs + order[i], CHUNK)], from_core.at[i], core_send.at[i], core_recv.at[i], other)
    wait(g_in, local_sem.at[1])
    for i in range(4):
        product(own + order[i])
    for i in range(4):
        wait(from_core.at[i], core_recv.at[i])
        here = rows(own + order[i], CHUNK)
        part[here, :] = part[here, :] + from_core[i]
        for j in range(4):
            if (i, j) != (0, 0):
                px, py = plane(i, j)
                src = part.at[rows(own + (py * 4 + px) * BLOCK, BLOCK)]
                send(src, plane_in.at[mine], send_sem.at[0], recv_sem.at[0], device(px, py, z, core))
    comb_copy = pltpu.make_async_copy(comb, comb_out, local_sem.at[2])
    comb_copy.start()
    plane_in[mine] = part[rows(own + mine * BLOCK, BLOCK), :]
    wait(plane_in.at[0:15], recv_sem.at[0])
    total = plane_in[0]
    for n in range(1, 16):
        total = total + plane_in[n]
    plane_sum[...] = total

    for o in (2, 1, 3):
        send(plane_sum.at[rows(near_at(o) * PART, PART)], near_in.at[near], send_sem.at[1], recv_sem.at[1], near_device(o))
    for n, (c, i) in enumerate(mate_offsets):
        index, to = mate(c, i)
        send(comb.at[rows(index * CHUNK, CHUNK)], mates.at[n], send_sem.at[2], recv_sem.at[2], to)
    near_in[near] = plane_sum[rows(near * PART, PART), :]
    wait(near_in.at[0:3], recv_sem.at[1])
    near_sum[...] = ((near_in[0] + near_in[1]) + near_in[2]) + near_in[3]

    for n, o in enumerate(ring_offsets):
        send(near_sum, far_in.at[far], far_send.at[n], far_recv.at[n], in_ring(o))
    far_in[far] = near_sum[...]
    above, below = far_in.at[(far + 2) & 7], far_in.at[(far - 2) & 7]
    wait(near_sum, far_recv.at[1])
    send(above, above, far_send.at[4], far_recv.at[4], in_ring(-2))
    send(above, above, far_send.at[5], far_recv.at[5], in_ring(-1))
    wait(near_sum, far_recv.at[0])
    send(below, below, far_send.at[6], far_recv.at[6], in_ring(1))
    for n in (2, 3, 5, 6, 4):
        wait(near_sum, far_recv.at[n])
    total = far_in[0]
    for n in range(1, 8):
        total = total + far_in[n]
    slab = own + y * CHUNK
    piece = full.at[rows(slab + x * BLOCK + near * PART, PART)]
    piece[...] = total * (1.0 / replicas)
    for o in (2, 1, 3, 0):
        for j in (2, 1, 3, 0):
            if (o, j) != (0, 0):
                send(piece, piece, send_sem.at[3], recv_sem.at[3], near_device(o, j))
    wait(mates.at[0:7], recv_sem.at[2])
    wait(full.at[0 : 15 * PART], recv_sem.at[3])

    value = jnp.concatenate(split(full[rows(slab, CHUNK), :]), axis=1)
    total = lax.dot_general(value, comb[rows(slab, CHUNK), :], (((0,), (0,)), ((), ())), preferred_element_type=F32)
    for n in range(7):
        total = total + lax.dot_general(value, mates[n], (((0,), (0,)), ((), ())), preferred_element_type=F32)
    right[...] = (total[0:64, 0:COLS] + total[128:192, 0:COLS]) + (total[64:128, COLS:] + total[192:256, COLS:])
    for n, (c, i) in enumerate(mate_offsets):
        index, to = mate(c, i)
        send(right.at[rows(index * 8, 8)], right_in.at[n], send_sem.at[4], recv_sem.at[4], to)
    piece = full.at[rows(slab, CHUNK)]
    for i in (2, 1, 3):
        send(piece, piece, send_sem.at[5], recv_sem.at[5], device(x, (y + i) & 3, z, core))
    lot = rows((core * 4 + y) * 8, 8)
    wait(right_in, recv_sem.at[4])
    total = right[lot, :]
    for n in range(7):
        total = total + right_in[n]
    right_near_sum[0] = total
    for o in (2, 1, 3):
        send(right_near_sum.at[0], right_near.at[near], send_sem.at[6], recv_sem.at[6], near_device(o))
    right_near[near] = right_near_sum[0]
    wait(full.at[0 : 3 * CHUNK], recv_sem.at[5])
    half = full.at[rows(own, OWN)]
    send(half, half, core_send.at[4], core_recv.at[4], other)

    def gram_of(start):
        total = None
        for i in range(4):
            here = rows(start + i * CHUNK, CHUNK)
            value = jnp.concatenate(split(full[here, :]), axis=1)
            pieces[here, :] = value
            term = lax.dot_general(value, value, (((0,), (0,)), ((), ())), preferred_element_type=F32)
            total = term if total is None else total + term
        return total

    wait(right_near.at[0:3], recv_sem.at[6])
    right_near_sum[1] = ((right_near[0] + right_near[1]) + right_near[2]) + right_near[3]
    line = far & 3
    for o in (2, 1, 3):
        send(right_near_sum.at[1], right_far.at[line], send_sem.at[7], recv_sem.at[7], in_line(o))
    right_far[line] = right_near_sum[1]
    grams[core] = gram_of(own)
    wait(half, core_recv.at[4])
    grams[1 - core] = gram_of(theirs)
    gram = grams[0] + grams[1]
    gram = (gram[0:128, 0:128] + gram[128:256, 128:256]) + (gram[0:128, 128:256] + gram[128:256, 0:128])
    gram = gram[0:RANK, :] + pltpu.roll(gram[RANK:128, :], RANK, 1)
    factor = inverse_factor(jnp.where(lanes < RANK, gram, jnp.where(lanes == at + RANK, 1.0, 0.0)))
    inverse = jnp.where(lanes < RANK, 0.0, factor)
    left_inverse = pltpu.roll(inverse, RANK, 1)

    wait(right_far.at[0:3], recv_sem.at[7])
    total = ((right_far[0] + right_far[1]) + right_far[2]) + right_far[3]
    piece = right_full.at[lot]
    piece[...] = total * (1.0 / replicas)
    for c, i in mate_offsets:
        send(piece, piece, send_sem.at[8], recv_sem.at[8], mate(c, i)[1])

    high, low = split(jnp.concatenate([left_inverse, inverse], axis=0))
    weights = jnp.concatenate([jnp.concatenate([high, high], axis=1), jnp.concatenate([low, low], axis=1)], axis=0)
    for i in range(HALF // CHUNK):
        here = pl.ds(i * CHUNK, CHUNK)
        value = lax.dot_general(pieces[here, :], weights, (((1,), (1,)), ((), ())), preferred_element_type=F32)
        q[here, :] = (value[:, 0:128] + value[:, 128:256]).astype(BF16)
    q_copy = pltpu.make_async_copy(q, q_out, local_sem.at[3])
    q_copy.start()
    wait(right_full.at[0:56], recv_sem.at[8])
    right_out[...] = jnp.dot(
        left_inverse[:, 0:RANK], right_full[...], precision=lax.Precision.HIGHEST, preferred_element_type=F32
    )

    for i in range(4):
        wait(from_core.at[i], core_send.at[i])
    wait(half, core_send.at[4])
    wait(plane_in.at[0:15], send_sem.at[0])
    wait(near_in.at[0:3], send_sem.at[1])
    wait(mates.at[0:7], send_sem.at[2])
    wait(full.at[0 : 15 * PART], send_sem.at[3])
    wait(right_in, send_sem.at[4])
    wait(full.at[0 : 3 * CHUNK], send_sem.at[5])
    wait(right_near.at[0:3], send_sem.at[6])
    wait(right_near.at[0:3], send_sem.at[7])
    wait(right_in, send_sem.at[8])
    for n in range(7):
        wait(near_sum, far_send.at[n])
    comb_copy.wait()
    q_copy.wait()


def finish_kernel(q, comb, right, approx, new_errors, approx_out, errors_out, sem):
    weights = twice(right[...].astype(BF16))
    copies = []
    for i in range(HALF // 512):
        here = pl.ds(i * 512, 512)
        full = jnp.dot(q[here, :], weights, preferred_element_type=F32)
        error = (comb[here, :].astype(F32) - full).astype(BF16)
        full = full.astype(BF16)
        for n in range(2):
            approx_out[n, here, :] = full[:, COLS * n : COLS * (n + 1)]
            errors_out[n, here, :] = error[:, COLS * n : COLS * (n + 1)]
        for n, (src, dst) in enumerate(((approx_out, approx), (errors_out, new_errors))):
            copies.append(pltpu.make_async_copy(src.at[:, here], dst.at[:, here], sem.at[n, i]))
            copies[-1].start()
    for copy in copies:
        copy.wait()


def local(replicas, grads, errors, basis):
    vmem, dma = pltpu.VMEM, pltpu.SemaphoreType.DMA
    anywhere, inside = pl.BlockSpec(memory_space=pl.ANY), pl.BlockSpec(memory_space=vmem)
    q, comb, right = pl.pallas_call(
        functools.partial(exchange_kernel, replicas),
        name="exchange",
        out_shape=(
            jax.ShapeDtypeStruct((HALF, 128), BF16),
            jax.ShapeDtypeStruct((HALF, 2 * COLS), BF16),
            jax.ShapeDtypeStruct((RANK, COLS), F32),
        ),
        in_specs=[pl.BlockSpec(memory_space=pltpu.HBM)] * 2 + [inside],
        out_specs=(anywhere, anywhere, inside),
        scratch_shapes=[
            vmem((2 * HALF, COLS), BF16), vmem((2 * HALF, COLS), BF16), vmem((HALF, 2 * COLS), BF16),
            vmem((128, 2 * COLS), BF16), vmem((HALF, 128), F32), vmem((4, CHUNK, 128), F32),
            vmem((16, BLOCK, 128), F32), vmem((BLOCK, 128), F32), vmem((4, PART, 128), F32), vmem((PART, 128), F32),
            vmem((8, PART, 128), F32), vmem((HALF, 128), F32), vmem((7, CHUNK, 2 * COLS), BF16),
            vmem((HALF, 256), BF16), vmem((2, 256, 256), F32), vmem((HALF, 128), BF16),
            vmem((RANK, COLS), F32), vmem((7, 8, COLS), F32), vmem((4, 8, COLS), F32),
            vmem((2, 8, COLS), F32), vmem((4, 8, COLS), F32), vmem((RANK, COLS), F32),
            dma((4,)), dma((5,)), dma((5,)), dma((9,)), dma((9,)), dma((7,)), dma((7,)),
        ],
        compiler_params=pltpu.CompilerParams(collective_id=0, has_side_effects=True, vmem_limit_bytes=20 << 20),
    )(grads, errors, basis.T)
    approx, new_errors = pl.pallas_call(
        finish_kernel,
        name="finish",
        out_shape=(jax.ShapeDtypeStruct((2, HALF, COLS), BF16),) * 2,
        in_specs=[inside] * 3,
        out_specs=(anywhere,) * 2,
        scratch_shapes=[vmem((2, HALF, COLS), BF16), vmem((2, HALF, COLS), BF16), dma((2, 4))],
        compiler_params=pltpu.CompilerParams(vmem_limit_bytes=16 << 20),
    )(q, comb, right)
    return approx.reshape(2 * HALF, COLS), new_errors.reshape(1, 2 * HALF, COLS), right.T


def solution(mesh):
    placed = (P("dp", None, "tensor"), P("dp", None, "tensor"), P("tensor", None))
    return jax.shard_map(
        functools.partial(local, mesh.shape["dp"]),
        mesh=mesh,
        in_specs=placed,
        out_specs=(P(None, "tensor"), P("dp", None, "tensor"), P("tensor", None)),
        check_vma=False,
    )
```

```python
import functools

import jax
import jax.numpy as jnp
from jax import lax
from jax.experimental import pallas as pl
from jax.experimental.pallas import tpu as pltpu
from jax.sharding import PartitionSpec as P

MESH = pl.DeviceIdType.MESH
F32, BF16 = jnp.float32, jnp.bfloat16
COLS, RANK = 128, 64
HALF = 2048
OWN = 1024
BLOCK = 64
PART = 16
CHUNK = 256


def device(x, y, z, core):
    return ((z & 15) * 8 + y * 2 + core, (z >> 4) * 4 + x)


def rows(start, size):
    return pl.ds(pl.multiple_of(start, size), size)


def send(src, dst, send_sem, recv_sem, to):
    copy = pltpu.make_async_remote_copy(
        src_ref=src, dst_ref=dst, send_sem=send_sem, recv_sem=recv_sem, device_id=to, device_id_type=MESH
    )
    copy.start()


def wait(ref, sem):
    pltpu.make_async_copy(ref, ref, sem).wait()


def split(value):
    high = value.astype(BF16)
    low = (value - high.astype(F32)).astype(BF16)
    return high, low


def twice(value):
    zeros = jnp.zeros_like(value)
    return jnp.concatenate(
        [jnp.concatenate([value, zeros], axis=1), jnp.concatenate([zeros, value], axis=1)], axis=0
    )


def inverse_factor(gram):
    tiles = RANK // 8
    rows_at = lax.broadcasted_iota(jnp.int32, (8, 128), 0)
    m = [gram[8 * b : 8 * b + 8, :] for b in range(tiles)]
    pivots = []
    for k in range(RANK):
        at, sub = divmod(k, 8)
        pivot_row = m[at][sub : sub + 1, :]
        pivot = pivot_row[:, k : k + 1]
        pivots.append(pivot)
        scaled = pivot_row * (1.0 / pivot)
        for b in range(at, tiles):
            update = m[b][:, k : k + 1] * scaled
            if b == at:
                update = jnp.where(rows_at > sub, update, 0.0)
            m[b] = m[b] - update
    out = []
    for b in range(tiles):
        scale = jnp.concatenate(pivots[8 * b : 8 * b + 8], axis=0)
        out.append(m[b] * lax.rsqrt(scale))
    return jnp.concatenate(out, axis=0)


def exchange_kernel(
    replicas, grads, errors, basis, q_out, comb_out, right_out,
    g_in, e_in, comb, blocks, part, from_core, plane_in, plane_sum, near_in, near_sum, far_in, full, mates, pieces, grams,
    q, right, right_in, right_near, right_near_sum, right_far, right_full,
    local_sem, core_send, core_recv, send_sem, recv_sem, far_send, far_recv, tokens,
):
    d, t = lax.axis_index("dp"), lax.axis_index("tensor")
    core, y, z, x = d & 1, (d >> 1) & 3, (t >> 2) * 16 + (d >> 3), t & 3
    near, far, mine = z & 3, z >> 2, y * 4 + x
    other = device(x, y, z, 1 - core)
    own, theirs = core * OWN, (1 - core) * OWN

    def plane(i, j):
        return (x + j) & 3, (y + i) & 3

    def near_at(o):
        return (near + o) & 3

    def near_device(o, j=0):
        return device((x + j) & 3, y, (z & 28) | near_at(o), core)

    def in_line(o):
        return device(x, y, (z & 19) | (((far + o) & 3) << 2), core)

    def in_ring(o):
        return device(x, y, (z + 4 * o) & 31, core)

    def mate(c, i):
        to_core, to_y = core ^ c, (y + i) & 3
        return to_core * 4 + to_y, device(x, to_y, z, to_core)

    offsets = [(i, j) for i in range(4) for j in range(4) if (i, j) != (0, 0)]
    mate_offsets = [(0, 2), (1, 2), (0, 1), (0, 3), (1, 1), (1, 3), (1, 0)]
    ring_offsets = [2, -2, 1, -1]

    for n, start in enumerate((theirs, own)):
        for base in (0, HALF):
            here = rows(base + start, OWN)
            pltpu.make_async_copy(grads.at[0, here], g_in.at[here], local_sem.at[n]).start()
            pltpu.make_async_copy(errors.at[0, here], e_in.at[here], local_sem.at[n]).start()

    def along(o):
        return device(x, y, (z + o) & 31, core)

    def signal(sem, partners):
        for to in partners:
            pl.semaphore_signal(sem, inc=1, device_id=to, device_id_type=MESH)

    barrier = pltpu.get_barrier_semaphore()
    line_x = [device(*plane(0, j), z, core) for j in (2, 1, 3)]
    line_y = [device(*plane(i, 0), z, core) for i in (2, 1, 3)]
    signal(barrier, line_x + line_y + [along(1), along(31), other])

    blocks[...] = twice(basis[...].astype(BF16))
    lanes = lax.broadcasted_iota(jnp.int32, (RANK, 128), 1)
    at = lax.broadcasted_iota(jnp.int32, (RANK, 128), 0)

    def product(start):
        both = []
        for base in (0, HALF):
            here = rows(base + start, CHUNK)
            both.append((g_in[here, :].astype(F32) + e_in[here, :].astype(F32)).astype(BF16))
        value = jnp.concatenate(both, axis=1)
        comb[rows(start, CHUNK), :] = value
        part[rows(start, CHUNK), :] = lax.dot_general(
            value, blocks[...], (((1,), (1,)), ((), ())), preferred_element_type=F32
        )

    order = [((y + i) & 3) * CHUNK for i in range(4)]
    wait(g_in, local_sem.at[0])
    for i in range(4):
        product(theirs + order[i])
    pl.semaphore_wait(barrier, 9)
    signal(tokens.at[0], line_x)
    signal(tokens.at[1], [along(1), along(31)])
    for i in range(4):
        send(part.at[rows(theirs + order[i], CHUNK)], from_core.at[i], core_send.at[i], core_recv.at[i], other)
    wait(g_in, local_sem.at[1])
    for i in range(4):
        product(own + order[i])
    pl.semaphore_wait(tokens.at[0], 3)
    pl.semaphore_wait(tokens.at[1], 2)
    signal(tokens.at[2], [along(2), along(30)])
    for i in range(4):
        wait(from_core.at[i], core_recv.at[i])
        here = rows(own + order[i], CHUNK)
        part[here, :] = part[here, :] + from_core[i]
        for j in range(4):
            if (i, j) != (0, 0):
                px, py = plane(i, j)
                src = part.at[rows(own + (py * 4 + px) * BLOCK, BLOCK)]
                send(src, plane_in.at[mine], send_sem.at[0], recv_sem.at[0], device(px, py, z, core))
    comb_copy = pltpu.make_async_copy(comb, comb_out, local_sem.at[2])
    comb_copy.start()
    plane_in[mine] = part[rows(own + mine * BLOCK, BLOCK), :]
    pl.semaphore_wait(tokens.at[2], 2)
    signal(tokens.at[3], [along(4), along(28)])
    wait(plane_in.at[0:15], recv_sem.at[0])
    total = plane_in[0]
    for n in range(1, 16):
        total = total + plane_in[n]
    plane_sum[...] = total

    for o in (2, 1, 3):
        send(plane_sum.at[rows(near_at(o) * PART, PART)], near_in.at[near], send_sem.at[1], recv_sem.at[1], near_device(o))
    for n, (c, i) in enumerate(mate_offsets):
        index, to = mate(c, i)
        send(comb.at[rows(index * CHUNK, CHUNK)], mates.at[n], send_sem.at[2], recv_sem.at[2], to)
    near_in[near] = plane_sum[rows(near * PART, PART), :]
    wait(near_in.at[0:3], recv_sem.at[1])
    near_sum[...] = ((near_in[0] + near_in[1]) + near_in[2]) + near_in[3]

    pl.semaphore_wait(tokens.at[3], 2)
    for n, o in enumerate(ring_offsets):
        send(near_sum, far_in.at[far], far_send.at[n], far_recv.at[n], in_ring(o))
    far_in[far] = near_sum[...]
    above, below = far_in.at[(far + 2) & 7], far_in.at[(far - 2) & 7]
    wait(near_sum, far_recv.at[1])
    send(above, above, far_send.at[4], far_recv.at[4], in_ring(-2))
    send(above, above, far_send.at[5], far_recv.at[5], in_ring(-1))
    wait(near_sum, far_recv.at[0])
    send(below, below, far_send.at[6], far_recv.at[6], in_ring(1))
    for n in (2, 3, 5, 6, 4):
        wait(near_sum, far_recv.at[n])
    total = far_in[0]
    for n in range(1, 8):
        total = total + far_in[n]
    slab = own + y * CHUNK
    piece = full.at[rows(slab + x * BLOCK + near * PART, PART)]
    piece[...] = total * (1.0 / replicas)
    for o in (2, 1, 3, 0):
        for j in (2, 1, 3, 0):
            if (o, j) != (0, 0):
                send(piece, piece, send_sem.at[3], recv_sem.at[3], near_device(o, j))
    wait(mates.at[0:7], recv_sem.at[2])
    wait(full.at[0 : 15 * PART], recv_sem.at[3])

    value = jnp.concatenate(split(full[rows(slab, CHUNK), :]), axis=1)
    total = lax.dot_general(value, comb[rows(slab, CHUNK), :], (((0,), (0,)), ((), ())), preferred_element_type=F32)
    for n in range(7):
        total = total + lax.dot_general(value, mates[n], (((0,), (0,)), ((), ())), preferred_element_type=F32)
    right[...] = (total[0:64, 0:COLS] + total[128:192, 0:COLS]) + (total[64:128, COLS:] + total[192:256, COLS:])
    for n, (c, i) in enumerate(mate_offsets):
        index, to = mate(c, i)
        send(right.at[rows(index * 8, 8)], right_in.at[n], send_sem.at[4], recv_sem.at[4], to)
    piece = full.at[rows(slab, CHUNK)]
    for i in (2, 1, 3):
        send(piece, piece, send_sem.at[5], recv_sem.at[5], device(x, (y + i) & 3, z, core))
    lot = rows((core * 4 + y) * 8, 8)
    wait(right_in, recv_sem.at[4])
    total = right[lot, :]
    for n in range(7):
        total = total + right_in[n]
    right_near_sum[0] = total
    for o in (2, 1, 3):
        send(right_near_sum.at[0], right_near.at[near], send_sem.at[6], recv_sem.at[6], near_device(o))
    right_near[near] = right_near_sum[0]
    wait(full.at[0 : 3 * CHUNK], recv_sem.at[5])
    half = full.at[rows(own, OWN)]
    send(half, half, core_send.at[4], core_recv.at[4], other)

    def gram_of(start):
        total = None
        for i in range(4):
            here = rows(start + i * CHUNK, CHUNK)
            value = jnp.concatenate(split(full[here, :]), axis=1)
            pieces[here, :] = value
            term = lax.dot_general(value, value, (((0,), (0,)), ((), ())), preferred_element_type=F32)
            total = term if total is None else total + term
        return total

    wait(right_near.at[0:3], recv_sem.at[6])
    right_near_sum[1] = ((right_near[0] + right_near[1]) + right_near[2]) + right_near[3]
    line = far & 3
    for o in (2, 1, 3):
        send(right_near_sum.at[1], right_far.at[line], send_sem.at[7], recv_sem.at[7], in_line(o))
    right_far[line] = right_near_sum[1]
    grams[core] = gram_of(own)
    wait(half, core_recv.at[4])
    grams[1 - core] = gram_of(theirs)
    gram = grams[0] + grams[1]
    gram = (gram[0:128, 0:128] + gram[128:256, 128:256]) + (gram[0:128, 128:256] + gram[128:256, 0:128])
    gram = gram[0:RANK, :] + pltpu.roll(gram[RANK:128, :], RANK, 1)
    factor = inverse_factor(jnp.where(lanes < RANK, gram, jnp.where(lanes == at + RANK, 1.0, 0.0)))
    inverse = jnp.where(lanes < RANK, 0.0, factor)
    left_inverse = pltpu.roll(inverse, RANK, 1)

    wait(right_far.at[0:3], recv_sem.at[7])
    total = ((right_far[0] + right_far[1]) + right_far[2]) + right_far[3]
    piece = right_full.at[lot]
    piece[...] = total * (1.0 / replicas)
    for c, i in mate_offsets:
        send(piece, piece, send_sem.at[8], recv_sem.at[8], mate(c, i)[1])

    high, low = split(jnp.concatenate([left_inverse, inverse], axis=0))
    weights = jnp.concatenate([jnp.concatenate([high, high], axis=1), jnp.concatenate([low, low], axis=1)], axis=0)
    for i in range(HALF // CHUNK):
        here = pl.ds(i * CHUNK, CHUNK)
        value = lax.dot_general(pieces[here, :], weights, (((1,), (1,)), ((), ())), preferred_element_type=F32)
        q[here, :] = (value[:, 0:128] + value[:, 128:256]).astype(BF16)
    q_copy = pltpu.make_async_copy(q, q_out, local_sem.at[3])
    q_copy.start()
    wait(right_full.at[0:56], recv_sem.at[8])
    right_out[...] = jnp.dot(
        left_inverse[:, 0:RANK], right_full[...], precision=lax.Precision.HIGHEST, preferred_element_type=F32
    )

    for i in range(4):
        wait(from_core.at[i], core_send.at[i])
    wait(half, core_send.at[4])
    wait(plane_in.at[0:15], send_sem.at[0])
    wait(near_in.at[0:3], send_sem.at[1])
    wait(mates.at[0:7], send_sem.at[2])
    wait(full.at[0 : 15 * PART], send_sem.at[3])
    wait(right_in, send_sem.at[4])
    wait(full.at[0 : 3 * CHUNK], send_sem.at[5])
    wait(right_near.at[0:3], send_sem.at[6])
    wait(right_near.at[0:3], send_sem.at[7])
    wait(right_in, send_sem.at[8])
    for n in range(7):
        wait(near_sum, far_send.at[n])
    comb_copy.wait()
    q_copy.wait()


def finish_kernel(q, comb, right, approx, new_errors, new_basis, approx_out, errors_out, sem, basis_sem):
    weights = twice(right[...].astype(BF16))
    copies = [pltpu.make_async_copy(right, new_basis, basis_sem)]
    copies[0].start()
    for i in range(HALF // 512):
        here = pl.ds(i * 512, 512)
        full = jnp.dot(q[here, :], weights, preferred_element_type=F32)
        error = (comb[here, :].astype(F32) - full).astype(BF16)
        full = full.astype(BF16)
        for n in range(2):
            approx_out[n, here, :] = full[:, COLS * n : COLS * (n + 1)]
            errors_out[n, here, :] = error[:, COLS * n : COLS * (n + 1)]
        for n, (src, dst) in enumerate(((approx_out, approx), (errors_out, new_errors))):
            copies.append(pltpu.make_async_copy(src.at[:, here], dst.at[:, here], sem.at[n, i]))
            copies[-1].start()
    for copy in copies:
        copy.wait()


def local(replicas, grads, errors, basis):
    vmem, dma = pltpu.VMEM, pltpu.SemaphoreType.DMA
    anywhere, inside = pl.BlockSpec(memory_space=pl.ANY), pl.BlockSpec(memory_space=vmem)
    q, comb, right = pl.pallas_call(
        functools.partial(exchange_kernel, replicas),
        name="exchange",
        out_shape=(
            jax.ShapeDtypeStruct((HALF, 128), BF16),
            jax.ShapeDtypeStruct((HALF, 2 * COLS), BF16),
            jax.ShapeDtypeStruct((RANK, COLS), F32),
        ),
        in_specs=[anywhere] * 2 + [inside],
        out_specs=(anywhere, anywhere, inside),
        scratch_shapes=[
            vmem((2 * HALF, COLS), BF16), vmem((2 * HALF, COLS), BF16), vmem((HALF, 2 * COLS), BF16),
            vmem((128, 2 * COLS), BF16), vmem((HALF, 128), F32), vmem((4, CHUNK, 128), F32),
            vmem((16, BLOCK, 128), F32), vmem((BLOCK, 128), F32), vmem((4, PART, 128), F32), vmem((PART, 128), F32),
            vmem((8, PART, 128), F32), vmem((HALF, 128), F32), vmem((7, CHUNK, 2 * COLS), BF16),
            vmem((HALF, 256), BF16), vmem((2, 256, 256), F32), vmem((HALF, 128), BF16),
            vmem((RANK, COLS), F32), vmem((7, 8, COLS), F32), vmem((4, 8, COLS), F32),
            vmem((2, 8, COLS), F32), vmem((4, 8, COLS), F32), vmem((RANK, COLS), F32),
            dma((4,)), dma((5,)), dma((5,)), dma((9,)), dma((9,)), dma((7,)), dma((7,)),
            pltpu.SemaphoreType.REGULAR((4,)),
        ],
        compiler_params=pltpu.CompilerParams(collective_id=0, has_side_effects=True, vmem_limit_bytes=52 << 20),
    )(grads, errors, basis.T)
    approx, new_errors, new_basis = pl.pallas_call(
        finish_kernel,
        name="finish",
        out_shape=(jax.ShapeDtypeStruct((2, HALF, COLS), BF16),) * 2 + (jax.ShapeDtypeStruct((RANK, COLS), F32),),
        in_specs=[inside] * 3,
        out_specs=(anywhere,) * 3,
        scratch_shapes=[vmem((2, HALF, COLS), BF16), vmem((2, HALF, COLS), BF16), dma((2, 4)), dma],
        compiler_params=pltpu.CompilerParams(vmem_limit_bytes=16 << 20),
    )(q, comb, right)
    return approx.reshape(2 * HALF, COLS), new_errors.reshape(1, 2 * HALF, COLS), new_basis.T


def solution(mesh):
    placed = (P("dp", None, "tensor"), P("dp", None, "tensor"), P("tensor", None))
    return jax.shard_map(
        functools.partial(local, mesh.shape["dp"]),
        mesh=mesh,
        in_specs=placed,
        out_specs=(P(None, "tensor"), P("dp", None, "tensor"), P("tensor", None)),
        check_vma=False,
    )
```

```python
import functools

import jax
import jax.numpy as jnp
from jax import lax
from jax.experimental import pallas as pl
from jax.experimental.pallas import tpu as pltpu
from jax.sharding import PartitionSpec as P

MESH = pl.DeviceIdType.MESH
F32, BF16 = jnp.float32, jnp.bfloat16
COLS, RANK = 128, 64
HALF = 2048
OWN = 1024
BLOCK = 64
PART = 16
CHUNK = 256


def device(x, y, z, core):
    return ((z & 15) * 8 + y * 2 + core, (z >> 4) * 4 + x)


def rows(start, size):
    return pl.ds(pl.multiple_of(start, size), size)


def send(src, dst, send_sem, recv_sem, to):
    copy = pltpu.make_async_remote_copy(
        src_ref=src, dst_ref=dst, send_sem=send_sem, recv_sem=recv_sem, device_id=to, device_id_type=MESH
    )
    copy.start()


def wait(ref, sem):
    pltpu.make_async_copy(ref, ref, sem).wait()


def split(value):
    high = value.astype(BF16)
    low = (value - high.astype(F32)).astype(BF16)
    return high, low


def twice(value):
    zeros = jnp.zeros_like(value)
    return jnp.concatenate(
        [jnp.concatenate([value, zeros], axis=1), jnp.concatenate([zeros, value], axis=1)], axis=0
    )


def inverse_factor(gram):
    tiles = RANK // 8
    rows_at = lax.broadcasted_iota(jnp.int32, (8, 128), 0)
    m = [gram[8 * b : 8 * b + 8, :] for b in range(tiles)]
    pivots = []
    for k in range(RANK):
        at, sub = divmod(k, 8)
        pivot_row = m[at][sub : sub + 1, :]
        pivot = pivot_row[:, k : k + 1]
        pivots.append(pivot)
        scaled = pivot_row * (1.0 / pivot)
        for b in range(at, tiles):
            update = m[b][:, k : k + 1] * scaled
            if b == at:
                update = jnp.where(rows_at > sub, update, 0.0)
            m[b] = m[b] - update
    out = []
    for b in range(tiles):
        scale = jnp.concatenate(pivots[8 * b : 8 * b + 8], axis=0)
        out.append(m[b] * lax.rsqrt(scale))
    return jnp.concatenate(out, axis=0)


def exchange_kernel(
    replicas, grads, errors, basis, q_out, comb_out, right_out,
    g_in, e_in, comb, blocks, part, from_core, plane_in, plane_sum, near_in, near_sum, far_in, full, mates, mate_sum, pieces, grams,
    q, right, right_in, right_sum, right_far, right_full,
    local_sem, core_send, core_recv, send_sem, recv_sem, far_send, far_recv, tokens,
):
    d, t = lax.axis_index("dp"), lax.axis_index("tensor")
    core, y, z, x = d & 1, (d >> 1) & 3, (t >> 2) * 16 + (d >> 3), t & 3
    near, far, mine = z & 3, z >> 2, y * 4 + x
    other = device(x, y, z, 1 - core)
    own, theirs = core * OWN, (1 - core) * OWN

    def plane(i, j):
        return (x + j) & 3, (y + i) & 3

    def near_at(o):
        return (near + o) & 3

    def near_device(o, j=0):
        return device((x + j) & 3, y, (z & 28) | near_at(o), core)

    def in_line(o):
        return device(x, y, (z & 19) | (((far + o) & 3) << 2), core)

    def in_ring(o):
        return device(x, y, (z + 4 * o) & 31, core)

    def mate(c, i):
        to_core, to_y = core ^ c, (y + i) & 3
        return to_core * 4 + to_y, device(x, to_y, z, to_core)

    offsets = [(i, j) for i in range(4) for j in range(4) if (i, j) != (0, 0)]
    mate_offsets = [(0, 2), (1, 2), (0, 1), (0, 3), (1, 1), (1, 3), (1, 0)]
    ring_offsets = [2, -2, 1, -1]

    def along(o):
        return device(x, y, (z + o) & 31, core)

    def signal(sem, partners):
        for to in partners:
            pl.semaphore_signal(sem, inc=1, device_id=to, device_id_type=MESH)

    barrier = pltpu.get_barrier_semaphore()
    line_x = [device(*plane(0, j), z, core) for j in (2, 1, 3)]
    line_y = [device(*plane(i, 0), z, core) for i in (2, 1, 3)]
    signal(barrier, line_x + line_y + [along(1), along(31), other])
    for n, start in enumerate((theirs, own)):
        for base in (0, HALF):
            here = rows(base + start, OWN)
            pltpu.make_async_copy(grads.at[0, here], g_in.at[here], local_sem.at[n]).start()
            pltpu.make_async_copy(errors.at[0, here], e_in.at[here], local_sem.at[n]).start()

    blocks[...] = twice(basis[...].astype(BF16))
    lanes = lax.broadcasted_iota(jnp.int32, (RANK, 128), 1)
    at = lax.broadcasted_iota(jnp.int32, (RANK, 128), 0)

    def product(start):
        both = []
        for base in (0, HALF):
            here = rows(base + start, CHUNK)
            both.append((g_in[here, :].astype(F32) + e_in[here, :].astype(F32)).astype(BF16))
        value = jnp.concatenate(both, axis=1)
        comb[rows(start, CHUNK), :] = value
        part[rows(start, CHUNK), :] = lax.dot_general(
            value, blocks[...], (((1,), (1,)), ((), ())), preferred_element_type=F32
        )

    order = [((y + i) & 3) * CHUNK for i in range(4)]
    wait(g_in, local_sem.at[0])
    for i in range(4):
        product(theirs + order[i])
    pl.semaphore_wait(barrier, 9)
    signal(tokens.at[0], line_x)
    signal(tokens.at[1], [along(1), along(31)])
    for i in range(4):
        send(part.at[rows(theirs + order[i], CHUNK)], from_core.at[i], core_send.at[i], core_recv.at[i], other)
    wait(g_in, local_sem.at[1])
    for i in range(4):
        product(own + order[i])
    for i in range(4):
        wait(from_core.at[i], core_recv.at[i])
        here = rows(own + order[i], CHUNK)
        part[here, :] = part[here, :] + from_core[i]
        for j in range(4):
            if (i, j) != (0, 0):
                px, py = plane(i, j)
                src = part.at[rows(own + (py * 4 + px) * BLOCK, BLOCK)]
                send(src, plane_in.at[mine], send_sem.at[0], recv_sem.at[0], device(px, py, z, core))
        if i == 0:
            pl.semaphore_wait(tokens.at[0], 3)
            pl.semaphore_wait(tokens.at[1], 2)
            signal(tokens.at[2], [along(2), along(30)])
    comb_copy = pltpu.make_async_copy(comb, comb_out, local_sem.at[2])
    comb_copy.start()
    plane_in[mine] = part[rows(own + mine * BLOCK, BLOCK), :]
    pl.semaphore_wait(tokens.at[2], 2)
    signal(tokens.at[3], [along(4), along(28)])
    wait(plane_in.at[0:15], recv_sem.at[0])
    total = plane_in[0]
    for n in range(1, 16):
        total = total + plane_in[n]
    plane_sum[...] = total

    for o in (2, 1, 3):
        send(plane_sum.at[rows(near_at(o) * PART, PART)], near_in.at[near], send_sem.at[1], recv_sem.at[1], near_device(o))
    for n, (c, i) in enumerate(mate_offsets):
        index, to = mate(c, i)
        send(comb.at[rows(index * CHUNK, CHUNK)], mates.at[n], send_sem.at[2], recv_sem.at[2], to)
    near_in[near] = plane_sum[rows(near * PART, PART), :]
    wait(near_in.at[0:3], recv_sem.at[1])
    near_sum[...] = ((near_in[0] + near_in[1]) + near_in[2]) + near_in[3]

    pl.semaphore_wait(tokens.at[3], 2)
    for n, o in enumerate(ring_offsets):
        send(near_sum, far_in.at[far], far_send.at[n], far_recv.at[n], in_ring(o))
    far_in[far] = near_sum[...]
    above, below = far_in.at[(far + 2) & 7], far_in.at[(far - 2) & 7]
    wait(near_sum, far_recv.at[1])
    send(above, above, far_send.at[4], far_recv.at[4], in_ring(-2))
    send(above, above, far_send.at[5], far_recv.at[5], in_ring(-1))
    wait(near_sum, far_recv.at[0])
    send(below, below, far_send.at[6], far_recv.at[6], in_ring(1))
    slab = own + y * CHUNK
    wait(mates.at[0:7], recv_sem.at[2])
    for i in range(4):
        here = pl.ds(i * 64, 64)
        total = comb[rows(slab + i * 64, 64), :].astype(F32)
        for n in range(7):
            total = total + mates[n, here, :].astype(F32)
        mate_sum[here, 0 : 2 * COLS], mate_sum[here, 2 * COLS :] = split(total)
    for n in (2, 3, 5, 6, 4):
        wait(near_sum, far_recv.at[n])
    total = far_in[0]
    for n in range(1, 8):
        total = total + far_in[n]
    piece = full.at[rows(slab + x * BLOCK + near * PART, PART)]
    piece[...] = total * (1.0 / replicas)
    for o in (2, 1, 3, 0):
        for j in (2, 1, 3, 0):
            if (o, j) != (0, 0):
                send(piece, piece, send_sem.at[3], recv_sem.at[3], near_device(o, j))
    wait(full.at[0 : 15 * PART], recv_sem.at[3])

    value = jnp.concatenate(split(full[rows(slab, CHUNK), :]), axis=1)
    total = lax.dot_general(value, mate_sum[...], (((0,), (0,)), ((), ())), preferred_element_type=F32)
    total = total[:, 0 : 2 * COLS] + total[:, 2 * COLS :]
    right[...] = (total[0:64, 0:COLS] + total[128:192, 0:COLS]) + (total[64:128, COLS:] + total[192:256, COLS:])
    me, lot = core * 4 + y, rows((core * 4 + y) * 8, 8)
    for o in (2, 1, 3, 0):
        for c, i in mate_offsets + [(0, 0)]:
            if (o, c, i) != (0, 0, 0):
                to_core, to_y = core ^ c, (y + i) & 3
                to = device(x, to_y, (z & 28) | near_at(o), to_core)
                src = right.at[rows((to_core * 4 + to_y) * 8, 8)]
                send(src, right_in.at[near * 8 + me], send_sem.at[4], recv_sem.at[4], to)
    right_in[near * 8 + me] = right[lot, :]
    piece = full.at[rows(slab, CHUNK)]
    for i in (2, 1, 3):
        send(piece, piece, send_sem.at[5], recv_sem.at[5], device(x, (y + i) & 3, z, core))

    def gram_of(start):
        total = None
        for i in range(4):
            here = rows(start + i * CHUNK, CHUNK)
            value = jnp.concatenate(split(full[here, :]), axis=1)
            pieces[here, :] = value
            term = lax.dot_general(value, value, (((0,), (0,)), ((), ())), preferred_element_type=F32)
            total = term if total is None else total + term
        return total

    wait(full.at[0 : 3 * CHUNK], recv_sem.at[5])
    half = full.at[rows(own, OWN)]
    send(half, half, core_send.at[4], core_recv.at[4], other)
    grams[core] = gram_of(own)
    wait(right_in.at[0:31], recv_sem.at[4])
    total = right_in[0]
    for n in range(1, 32):
        total = total + right_in[n]
    right_sum[...] = total
    line = far & 3
    for o in (2, 1, 3):
        send(right_sum, right_far.at[line], send_sem.at[7], recv_sem.at[7], in_line(o))
    right_far[line] = right_sum[...]
    wait(half, core_recv.at[4])
    grams[1 - core] = gram_of(theirs)
    gram = grams[0] + grams[1]
    gram = (gram[0:128, 0:128] + gram[128:256, 128:256]) + (gram[0:128, 128:256] + gram[128:256, 0:128])
    gram = gram[0:RANK, :] + pltpu.roll(gram[RANK:128, :], RANK, 1)
    factor = inverse_factor(jnp.where(lanes < RANK, gram, jnp.where(lanes == at + RANK, 1.0, 0.0)))
    inverse = jnp.where(lanes < RANK, 0.0, factor)
    left_inverse = pltpu.roll(inverse, RANK, 1)

    wait(right_far.at[0:3], recv_sem.at[7])
    total = ((right_far[0] + right_far[1]) + right_far[2]) + right_far[3]
    piece = right_full.at[lot]
    piece[...] = total * (1.0 / replicas)
    for c, i in mate_offsets:
        send(piece, piece, send_sem.at[8], recv_sem.at[8], mate(c, i)[1])

    high, low = split(jnp.concatenate([left_inverse, inverse], axis=0))
    weights = jnp.concatenate([jnp.concatenate([high, high], axis=1), jnp.concatenate([low, low], axis=1)], axis=0)
    for i in range(HALF // CHUNK):
        here = pl.ds(i * CHUNK, CHUNK)
        value = lax.dot_general(pieces[here, :], weights, (((1,), (1,)), ((), ())), preferred_element_type=F32)
        q[here, :] = (value[:, 0:128] + value[:, 128:256]).astype(BF16)
    q_copy = pltpu.make_async_copy(q, q_out, local_sem.at[3])
    q_copy.start()
    wait(right_full.at[0:56], recv_sem.at[8])
    right_out[...] = jnp.dot(
        left_inverse[:, 0:RANK], right_full[...], precision=lax.Precision.HIGHEST, preferred_element_type=F32
    )

    for i in range(4):
        wait(from_core.at[i], core_send.at[i])
    wait(half, core_send.at[4])
    wait(plane_in.at[0:15], send_sem.at[0])
    wait(near_in.at[0:3], send_sem.at[1])
    wait(mates.at[0:7], send_sem.at[2])
    wait(full.at[0 : 15 * PART], send_sem.at[3])
    wait(right_in.at[0:31], send_sem.at[4])
    wait(full.at[0 : 3 * CHUNK], send_sem.at[5])
    wait(right_far.at[0:3], send_sem.at[7])
    wait(right_in.at[0:7], send_sem.at[8])
    for n in range(7):
        wait(near_sum, far_send.at[n])
    comb_copy.wait()
    q_copy.wait()


def finish_kernel(q, comb, right, approx, new_errors, new_basis, approx_out, errors_out, sem, basis_sem):
    weights = twice(right[...].astype(BF16))
    copies = [pltpu.make_async_copy(right, new_basis, basis_sem)]
    copies[0].start()
    for i in range(HALF // 512):
        here = pl.ds(i * 512, 512)
        full = jnp.dot(q[here, :], weights, preferred_element_type=F32)
        error = (comb[here, :].astype(F32) - full).astype(BF16)
        full = full.astype(BF16)
        for n in range(2):
            approx_out[n, here, :] = full[:, COLS * n : COLS * (n + 1)]
            errors_out[n, here, :] = error[:, COLS * n : COLS * (n + 1)]
        for n, (src, dst) in enumerate(((approx_out, approx), (errors_out, new_errors))):
            copies.append(pltpu.make_async_copy(src.at[:, here], dst.at[:, here], sem.at[n, i]))
            copies[-1].start()
    for copy in copies:
        copy.wait()


def local(replicas, grads, errors, basis):
    vmem, dma = pltpu.VMEM, pltpu.SemaphoreType.DMA
    anywhere, inside = pl.BlockSpec(memory_space=pl.ANY), pl.BlockSpec(memory_space=vmem)
    q, comb, right = pl.pallas_call(
        functools.partial(exchange_kernel, replicas),
        name="exchange",
        out_shape=(
            jax.ShapeDtypeStruct((HALF, 128), BF16),
            jax.ShapeDtypeStruct((HALF, 2 * COLS), BF16),
            jax.ShapeDtypeStruct((RANK, COLS), F32),
        ),
        in_specs=[anywhere] * 2 + [inside],
        out_specs=(anywhere, anywhere, inside),
        scratch_shapes=[
            vmem((2 * HALF, COLS), BF16), vmem((2 * HALF, COLS), BF16), vmem((HALF, 2 * COLS), BF16),
            vmem((128, 2 * COLS), BF16), vmem((HALF, 128), F32), vmem((4, CHUNK, 128), F32),
            vmem((16, BLOCK, 128), F32), vmem((BLOCK, 128), F32), vmem((4, PART, 128), F32), vmem((PART, 128), F32),
            vmem((8, PART, 128), F32), vmem((HALF, 128), F32), vmem((7, CHUNK, 2 * COLS), BF16),
            vmem((CHUNK, 4 * COLS), BF16),
            vmem((HALF, 256), BF16), vmem((2, 256, 256), F32), vmem((HALF, 128), BF16),
            vmem((RANK, COLS), F32), vmem((32, 8, COLS), F32), vmem((8, COLS), F32),
            vmem((4, 8, COLS), F32), vmem((RANK, COLS), F32),
            dma((4,)), dma((5,)), dma((5,)), dma((9,)), dma((9,)), dma((7,)), dma((7,)),
            pltpu.SemaphoreType.REGULAR((4,)),
        ],
        compiler_params=pltpu.CompilerParams(collective_id=0, has_side_effects=True, vmem_limit_bytes=52 << 20),
    )(grads, errors, basis.T)
    approx, new_errors, new_basis = pl.pallas_call(
        finish_kernel,
        name="finish",
        out_shape=(jax.ShapeDtypeStruct((2, HALF, COLS), BF16),) * 2 + (jax.ShapeDtypeStruct((RANK, COLS), F32),),
        in_specs=[inside] * 3,
        out_specs=(anywhere,) * 3,
        scratch_shapes=[vmem((2, HALF, COLS), BF16), vmem((2, HALF, COLS), BF16), dma((2, 4)), dma],
        compiler_params=pltpu.CompilerParams(vmem_limit_bytes=16 << 20),
    )(q, comb, right)
    return approx.reshape(2 * HALF, COLS), new_errors.reshape(1, 2 * HALF, COLS), new_basis.T


def solution(mesh):
    placed = (P("dp", None, "tensor"), P("dp", None, "tensor"), P("tensor", None))
    return jax.shard_map(
        functools.partial(local, mesh.shape["dp"]),
        mesh=mesh,
        in_specs=placed,
        out_specs=(P(None, "tensor"), P("dp", None, "tensor"), P("tensor", None)),
        check_vma=False,
    )
```

```python
import functools

import jax
import jax.numpy as jnp
from jax import lax
from jax.experimental import pallas as pl
from jax.experimental.pallas import tpu as pltpu
from jax.sharding import PartitionSpec as P

MESH = pl.DeviceIdType.MESH
F32, BF16 = jnp.float32, jnp.bfloat16
COLS, RANK = 128, 64
HALF = 2048
OWN = 1024
BLOCK = 64
PART = 16
CHUNK = 256


def device(x, y, z, core):
    return ((z & 15) * 8 + y * 2 + core, (z >> 4) * 4 + x)


def rows(start, size):
    return pl.ds(pl.multiple_of(start, size), size)


def send(src, dst, send_sem, recv_sem, to):
    copy = pltpu.make_async_remote_copy(
        src_ref=src, dst_ref=dst, send_sem=send_sem, recv_sem=recv_sem, device_id=to, device_id_type=MESH
    )
    copy.start()


def wait(ref, sem):
    pltpu.make_async_copy(ref, ref, sem).wait()


def split(value):
    high = value.astype(BF16)
    low = (value - high.astype(F32)).astype(BF16)
    return high, low


def twice(value):
    zeros = jnp.zeros_like(value)
    return jnp.concatenate(
        [jnp.concatenate([value, zeros], axis=1), jnp.concatenate([zeros, value], axis=1)], axis=0
    )


def inverse_factor(gram):
    tiles = RANK // 8
    rows_at = lax.broadcasted_iota(jnp.int32, (8, 128), 0)
    m = [gram[8 * b : 8 * b + 8, :] for b in range(tiles)]
    pivots = []
    for k in range(RANK):
        at, sub = divmod(k, 8)
        pivot_row = m[at][sub : sub + 1, :]
        pivot = pivot_row[:, k : k + 1]
        pivots.append(pivot)
        scaled = pivot_row * (1.0 / pivot)
        for b in range(at, tiles):
            update = m[b][:, k : k + 1] * scaled
            if b == at:
                update = jnp.where(rows_at > sub, update, 0.0)
            m[b] = m[b] - update
    out = []
    for b in range(tiles):
        scale = jnp.concatenate(pivots[8 * b : 8 * b + 8], axis=0)
        out.append(m[b] * lax.rsqrt(scale))
    return jnp.concatenate(out, axis=0)


def exchange_kernel(
    replicas, grads, errors, basis, q_out, comb_out, right_out,
    g_in, e_in, basis_in, comb, blocks, part, from_core, plane_in, plane_sum, near_in, near_sum, far_in, full, mates, mate_sum, pieces, grams,
    q, right, right_in, right_sum, right_far, right_full,
    local_sem, core_send, core_recv, send_sem, recv_sem, far_send, far_recv, tokens,
):
    d, t = lax.axis_index("dp"), lax.axis_index("tensor")
    core, y, z, x = d & 1, (d >> 1) & 3, (t >> 2) * 16 + (d >> 3), t & 3
    near, far, mine = z & 3, z >> 2, y * 4 + x
    other = device(x, y, z, 1 - core)
    own, theirs = core * OWN, (1 - core) * OWN

    def plane(i, j):
        return (x + j) & 3, (y + i) & 3

    def near_at(o):
        return (near + o) & 3

    def near_device(o, j=0):
        return device((x + j) & 3, y, (z & 28) | near_at(o), core)

    def in_line(o):
        return device(x, y, (z & 19) | (((far + o) & 3) << 2), core)

    def in_ring(o):
        return device(x, y, (z + 4 * o) & 31, core)

    def mate(c, i):
        to_core, to_y = core ^ c, (y + i) & 3
        return to_core * 4 + to_y, device(x, to_y, z, to_core)

    offsets = [(i, j) for i in range(4) for j in range(4) if (i, j) != (0, 0)]
    mate_offsets = [(0, 2), (1, 2), (0, 1), (0, 3), (1, 1), (1, 3), (1, 0)]
    ring_offsets = [2, -2, 1, -1]

    def along(o):
        return device(x, y, (z + o) & 31, core)

    def signal(sem, partners):
        for to in partners:
            pl.semaphore_signal(sem, inc=1, device_id=to, device_id_type=MESH)

    barrier = pltpu.get_barrier_semaphore()
    line_x = [device(*plane(0, j), z, core) for j in (2, 1, 3)]
    line_y = [device(*plane(i, 0), z, core) for i in (2, 1, 3)]
    signal(barrier, line_x + line_y + [along(1), along(31), other])
    pltpu.make_async_copy(basis, basis_in, local_sem.at[4]).start()
    for n, start in enumerate((theirs, own)):
        for base in (0, HALF):
            here = rows(base + start, OWN)
            pltpu.make_async_copy(grads.at[0, here], g_in.at[here], local_sem.at[n]).start()
            pltpu.make_async_copy(errors.at[0, here], e_in.at[here], local_sem.at[n]).start()

    wait(basis_in, local_sem.at[4])
    blocks[...] = twice(basis_in[...].astype(BF16))
    lanes = lax.broadcasted_iota(jnp.int32, (RANK, 128), 1)
    at = lax.broadcasted_iota(jnp.int32, (RANK, 128), 0)

    def product(start):
        both = []
        for base in (0, HALF):
            here = rows(base + start, CHUNK)
            both.append((g_in[here, :].astype(F32) + e_in[here, :].astype(F32)).astype(BF16))
        value = jnp.concatenate(both, axis=1)
        comb[rows(start, CHUNK), :] = value
        part[rows(start, CHUNK), :] = lax.dot_general(
            value, blocks[...], (((1,), (1,)), ((), ())), preferred_element_type=F32
        )

    order = [((y + i) & 3) * CHUNK for i in range(4)]
    wait(g_in, local_sem.at[0])
    for i in range(4):
        product(theirs + order[i])
    pl.semaphore_wait(barrier, 9)
    signal(tokens.at[0], line_x)
    signal(tokens.at[1], [along(1), along(31)])
    for i in range(4):
        send(part.at[rows(theirs + order[i], CHUNK)], from_core.at[i], core_send.at[i], core_recv.at[i], other)
    wait(g_in, local_sem.at[1])
    for i in range(4):
        product(own + order[i])
    for i in range(4):
        wait(from_core.at[i], core_recv.at[i])
        here = rows(own + order[i], CHUNK)
        part[here, :] = part[here, :] + from_core[i]
        for j in range(4):
            if (i, j) != (0, 0):
                px, py = plane(i, j)
                src = part.at[rows(own + (py * 4 + px) * BLOCK, BLOCK)]
                send(src, plane_in.at[mine], send_sem.at[0], recv_sem.at[0], device(px, py, z, core))
        if i == 0:
            pl.semaphore_wait(tokens.at[0], 3)
            pl.semaphore_wait(tokens.at[1], 2)
            signal(tokens.at[2], [along(2), along(30)])
    comb_copy = pltpu.make_async_copy(comb, comb_out, local_sem.at[2])
    comb_copy.start()
    plane_in[mine] = part[rows(own + mine * BLOCK, BLOCK), :]
    pl.semaphore_wait(tokens.at[2], 2)
    signal(tokens.at[3], [along(4), along(28)])
    wait(plane_in.at[0:15], recv_sem.at[0])
    total = plane_in[0]
    for n in range(1, 16):
        total = total + plane_in[n]
    plane_sum[...] = total

    for o in (2, 1, 3):
        send(plane_sum.at[rows(near_at(o) * PART, PART)], near_in.at[near], send_sem.at[1], recv_sem.at[1], near_device(o))
    for n, (c, i) in enumerate(mate_offsets):
        index, to = mate(c, i)
        send(comb.at[rows(index * CHUNK, CHUNK)], mates.at[n], send_sem.at[2], recv_sem.at[2], to)
    near_in[near] = plane_sum[rows(near * PART, PART), :]
    wait(near_in.at[0:3], recv_sem.at[1])
    near_sum[...] = ((near_in[0] + near_in[1]) + near_in[2]) + near_in[3]

    pl.semaphore_wait(tokens.at[3], 2)
    for n, o in enumerate(ring_offsets):
        send(near_sum, far_in.at[far], far_send.at[n], far_recv.at[n], in_ring(o))
    far_in[far] = near_sum[...]
    above, below = far_in.at[(far + 2) & 7], far_in.at[(far - 2) & 7]
    wait(near_sum, far_recv.at[1])
    send(above, above, far_send.at[4], far_recv.at[4], in_ring(-2))
    send(above, above, far_send.at[5], far_recv.at[5], in_ring(-1))
    wait(near_sum, far_recv.at[0])
    send(below, below, far_send.at[6], far_recv.at[6], in_ring(1))
    slab = own + y * CHUNK
    wait(mates.at[0:7], recv_sem.at[2])
    for i in range(4):
        here = pl.ds(i * 64, 64)
        total = comb[rows(slab + i * 64, 64), :].astype(F32)
        for n in range(7):
            total = total + mates[n, here, :].astype(F32)
        mate_sum[here, 0 : 2 * COLS], mate_sum[here, 2 * COLS :] = split(total)
    for n in (2, 3, 5, 6, 4):
        wait(near_sum, far_recv.at[n])
    total = far_in[0]
    for n in range(1, 8):
        total = total + far_in[n]
    piece = full.at[rows(slab + x * BLOCK + near * PART, PART)]
    piece[...] = total * (1.0 / replicas)
    for o in (2, 1, 3, 0):
        for j in (2, 1, 3, 0):
            if (o, j) != (0, 0):
                send(piece, piece, send_sem.at[3], recv_sem.at[3], near_device(o, j))
    wait(full.at[0 : 15 * PART], recv_sem.at[3])

    value = jnp.concatenate(split(full[rows(slab, CHUNK), :]), axis=1)
    total = lax.dot_general(value, mate_sum[...], (((0,), (0,)), ((), ())), preferred_element_type=F32)
    total = total[:, 0 : 2 * COLS] + total[:, 2 * COLS :]
    right[...] = (total[0:64, 0:COLS] + total[128:192, 0:COLS]) + (total[64:128, COLS:] + total[192:256, COLS:])
    me, lot = core * 4 + y, rows((core * 4 + y) * 8, 8)
    for o in (2, 1, 3, 0):
        for c, i in mate_offsets + [(0, 0)]:
            if (o, c, i) != (0, 0, 0):
                to_core, to_y = core ^ c, (y + i) & 3
                to = device(x, to_y, (z & 28) | near_at(o), to_core)
                src = right.at[rows((to_core * 4 + to_y) * 8, 8)]
                send(src, right_in.at[near * 8 + me], send_sem.at[4], recv_sem.at[4], to)
    right_in[near * 8 + me] = right[lot, :]
    piece = full.at[rows(slab, CHUNK)]
    for i in (2, 1, 3):
        send(piece, piece, send_sem.at[5], recv_sem.at[5], device(x, (y + i) & 3, z, core))

    def gram_of(start):
        total = None
        for i in range(4):
            here = rows(start + i * CHUNK, CHUNK)
            value = jnp.concatenate(split(full[here, :]), axis=1)
            pieces[here, :] = value
            term = lax.dot_general(value, value, (((0,), (0,)), ((), ())), preferred_element_type=F32)
            total = term if total is None else total + term
        return total

    wait(full.at[0 : 3 * CHUNK], recv_sem.at[5])
    half = full.at[rows(own, OWN)]
    send(half, half, core_send.at[4], core_recv.at[4], other)
    grams[core] = gram_of(own)
    wait(right_in.at[0:31], recv_sem.at[4])
    total = right_in[0]
    for n in range(1, 32):
        total = total + right_in[n]
    right_sum[...] = total
    line = far & 3
    for o in (2, 1, 3):
        send(right_sum, right_far.at[line], send_sem.at[7], recv_sem.at[7], in_line(o))
    right_far[line] = right_sum[...]
    wait(half, core_recv.at[4])
    grams[1 - core] = gram_of(theirs)
    gram = grams[0] + grams[1]
    gram = (gram[0:128, 0:128] + gram[128:256, 128:256]) + (gram[0:128, 128:256] + gram[128:256, 0:128])
    gram = gram[0:RANK, :] + pltpu.roll(gram[RANK:128, :], RANK, 1)
    factor = inverse_factor(jnp.where(lanes < RANK, gram, jnp.where(lanes == at + RANK, 1.0, 0.0)))
    inverse = jnp.where(lanes < RANK, 0.0, factor)
    left_inverse = pltpu.roll(inverse, RANK, 1)

    wait(right_far.at[0:3], recv_sem.at[7])
    total = ((right_far[0] + right_far[1]) + right_far[2]) + right_far[3]
    piece = right_full.at[lot]
    piece[...] = total * (1.0 / replicas)
    for c, i in mate_offsets:
        send(piece, piece, send_sem.at[8], recv_sem.at[8], mate(c, i)[1])

    high, low = split(jnp.concatenate([left_inverse, inverse], axis=0))
    weights = jnp.concatenate([jnp.concatenate([high, high], axis=1), jnp.concatenate([low, low], axis=1)], axis=0)
    for i in range(HALF // CHUNK):
        here = pl.ds(i * CHUNK, CHUNK)
        value = lax.dot_general(pieces[here, :], weights, (((1,), (1,)), ((), ())), preferred_element_type=F32)
        q[here, :] = (value[:, 0:128] + value[:, 128:256]).astype(BF16)
    q_copy = pltpu.make_async_copy(q, q_out, local_sem.at[3])
    q_copy.start()
    wait(right_full.at[0:56], recv_sem.at[8])
    right_out[...] = jnp.dot(
        left_inverse[:, 0:RANK], right_full[...], precision=lax.Precision.HIGHEST, preferred_element_type=F32
    )

    for i in range(4):
        wait(from_core.at[i], core_send.at[i])
    wait(half, core_send.at[4])
    wait(plane_in.at[0:15], send_sem.at[0])
    wait(near_in.at[0:3], send_sem.at[1])
    wait(mates.at[0:7], send_sem.at[2])
    wait(full.at[0 : 15 * PART], send_sem.at[3])
    wait(right_in.at[0:31], send_sem.at[4])
    wait(full.at[0 : 3 * CHUNK], send_sem.at[5])
    wait(right_far.at[0:3], send_sem.at[7])
    wait(right_in.at[0:7], send_sem.at[8])
    for n in range(7):
        wait(near_sum, far_send.at[n])
    comb_copy.wait()
    q_copy.wait()


def finish_kernel(q, comb, right, approx, new_errors, new_basis, approx_out, errors_out, sem, basis_sem):
    weights = twice(right[...].astype(BF16))
    copies = [pltpu.make_async_copy(right, new_basis, basis_sem)]
    copies[0].start()
    for i in range(HALF // 512):
        here = pl.ds(i * 512, 512)
        full = jnp.dot(q[here, :], weights, preferred_element_type=F32)
        error = (comb[here, :].astype(F32) - full).astype(BF16)
        full = full.astype(BF16)
        for n in range(2):
            approx_out[n, here, :] = full[:, COLS * n : COLS * (n + 1)]
            errors_out[n, here, :] = error[:, COLS * n : COLS * (n + 1)]
        for n, (src, dst) in enumerate(((approx_out, approx), (errors_out, new_errors))):
            copies.append(pltpu.make_async_copy(src.at[:, here], dst.at[:, here], sem.at[n, i]))
            copies[-1].start()
    for copy in copies:
        copy.wait()


def local(replicas, grads, errors, basis):
    vmem, dma = pltpu.VMEM, pltpu.SemaphoreType.DMA
    anywhere, inside = pl.BlockSpec(memory_space=pl.ANY), pl.BlockSpec(memory_space=vmem)
    q, comb, right = pl.pallas_call(
        functools.partial(exchange_kernel, replicas),
        name="exchange",
        out_shape=(
            jax.ShapeDtypeStruct((HALF, 128), BF16),
            jax.ShapeDtypeStruct((HALF, 2 * COLS), BF16),
            jax.ShapeDtypeStruct((RANK, COLS), F32),
        ),
        in_specs=[pl.BlockSpec(memory_space=pltpu.HBM)] * 3,
        out_specs=(anywhere, anywhere, inside),
        scratch_shapes=[
            vmem((2 * HALF, COLS), BF16), vmem((2 * HALF, COLS), BF16), vmem((RANK, COLS), F32), vmem((HALF, 2 * COLS), BF16),
            vmem((128, 2 * COLS), BF16), vmem((HALF, 128), F32), vmem((4, CHUNK, 128), F32),
            vmem((16, BLOCK, 128), F32), vmem((BLOCK, 128), F32), vmem((4, PART, 128), F32), vmem((PART, 128), F32),
            vmem((8, PART, 128), F32), vmem((HALF, 128), F32), vmem((7, CHUNK, 2 * COLS), BF16),
            vmem((CHUNK, 4 * COLS), BF16),
            vmem((HALF, 256), BF16), vmem((2, 256, 256), F32), vmem((HALF, 128), BF16),
            vmem((RANK, COLS), F32), vmem((32, 8, COLS), F32), vmem((8, COLS), F32),
            vmem((4, 8, COLS), F32), vmem((RANK, COLS), F32),
            dma((5,)), dma((5,)), dma((5,)), dma((9,)), dma((9,)), dma((7,)), dma((7,)),
            pltpu.SemaphoreType.REGULAR((4,)),
        ],
        compiler_params=pltpu.CompilerParams(collective_id=0, has_side_effects=True, vmem_limit_bytes=52 << 20),
    )(grads, errors, pltpu.with_memory_space_constraint(basis.T, pltpu.HBM))
    approx, new_errors, new_basis = pl.pallas_call(
        finish_kernel,
        name="finish",
        out_shape=(jax.ShapeDtypeStruct((2, HALF, COLS), BF16),) * 2 + (jax.ShapeDtypeStruct((RANK, COLS), F32),),
        in_specs=[inside] * 3,
        out_specs=(anywhere,) * 3,
        scratch_shapes=[vmem((2, HALF, COLS), BF16), vmem((2, HALF, COLS), BF16), dma((2, 4)), dma],
        compiler_params=pltpu.CompilerParams(vmem_limit_bytes=16 << 20),
    )(q, comb, right)
    return approx.reshape(2 * HALF, COLS), new_errors.reshape(1, 2 * HALF, COLS), new_basis.T


def solution(mesh):
    placed = (P("dp", None, "tensor"), P("dp", None, "tensor"), P("tensor", None))
    return jax.shard_map(
        functools.partial(local, mesh.shape["dp"]),
        mesh=mesh,
        in_specs=placed,
        out_specs=(P(None, "tensor"), P("dp", None, "tensor"), P("tensor", None)),
        check_vma=False,
    )
```

```python
import functools

import jax
import jax.numpy as jnp
from jax import lax
from jax.experimental import pallas as pl
from jax.experimental.pallas import tpu as pltpu
from jax.sharding import PartitionSpec as P

MESH = pl.DeviceIdType.MESH
F32, BF16 = jnp.float32, jnp.bfloat16
COLS, RANK = 128, 64
HALF = 2048
OWN = 1024
BLOCK = 64
PART = 16
CHUNK = 256


def device(x, y, z, core):
    return ((z & 15) * 8 + y * 2 + core, (z >> 4) * 4 + x)


def rows(start, size):
    return pl.ds(pl.multiple_of(start, size), size)


def send(src, dst, send_sem, recv_sem, to):
    copy = pltpu.make_async_remote_copy(
        src_ref=src, dst_ref=dst, send_sem=send_sem, recv_sem=recv_sem, device_id=to, device_id_type=MESH
    )
    copy.start()


def wait(ref, sem):
    pltpu.make_async_copy(ref, ref, sem).wait()


def split(value):
    high = value.astype(BF16)
    low = (value - high.astype(F32)).astype(BF16)
    return high, low


def twice(value):
    zeros = jnp.zeros_like(value)
    return jnp.concatenate(
        [jnp.concatenate([value, zeros], axis=1), jnp.concatenate([zeros, value], axis=1)], axis=0
    )


def inverse_factor(gram):
    tiles = RANK // 8
    rows_at = lax.broadcasted_iota(jnp.int32, (8, 128), 0)
    m = [gram[8 * b : 8 * b + 8, :] for b in range(tiles)]
    pivots = []
    for k in range(RANK):
        at, sub = divmod(k, 8)
        pivot_row = m[at][sub : sub + 1, :]
        pivot = pivot_row[:, k : k + 1]
        pivots.append(pivot)
        scaled = pivot_row * (1.0 / pivot)
        for b in range(at, tiles):
            update = m[b][:, k : k + 1] * scaled
            if b == at:
                update = jnp.where(rows_at > sub, update, 0.0)
            m[b] = m[b] - update
    out = []
    for b in range(tiles):
        scale = jnp.concatenate(pivots[8 * b : 8 * b + 8], axis=0)
        out.append(m[b] * lax.rsqrt(scale))
    return jnp.concatenate(out, axis=0)


def exchange_kernel(
    replicas, grads, errors, basis, q_out, comb_out, right_out,
    g_in, e_in, basis_in, comb, blocks, part, from_core, plane_in, plane_sum, near_in, near_sum, far_in, full, mates, mate_sum, pieces, grams,
    q, right, right_in, right_sum, right_far, right_full,
    local_sem, core_send, core_recv, send_sem, recv_sem, far_send, far_recv, tokens,
):
    d, t = lax.axis_index("dp"), lax.axis_index("tensor")
    core, y, z, x = d & 1, (d >> 1) & 3, (t >> 2) * 16 + (d >> 3), t & 3
    near, far, mine = z & 3, z >> 2, y * 4 + x
    other = device(x, y, z, 1 - core)
    own, theirs = core * OWN, (1 - core) * OWN

    def plane(i, j):
        return (x + j) & 3, (y + i) & 3

    def near_at(o):
        return (near + o) & 3

    def near_device(o, j=0):
        return device((x + j) & 3, y, (z & 28) | near_at(o), core)

    def in_line(o):
        return device(x, y, (z & 19) | (((far + o) & 3) << 2), core)

    def in_ring(o):
        return device(x, y, (z + 4 * o) & 31, core)

    def mate(c, i):
        to_core, to_y = core ^ c, (y + i) & 3
        return to_core * 4 + to_y, device(x, to_y, z, to_core)

    offsets = [(i, j) for i in range(4) for j in range(4) if (i, j) != (0, 0)]
    mate_offsets = [(0, 2), (1, 2), (0, 1), (0, 3), (1, 1), (1, 3), (1, 0)]
    ring_offsets = [2, -2, 1, -1]

    def along(o):
        return device(x, y, (z + o) & 31, core)

    def signal(sem, partners):
        for to in partners:
            pl.semaphore_signal(sem, inc=1, device_id=to, device_id_type=MESH)

    barrier = pltpu.get_barrier_semaphore()
    line_x = [device(*plane(0, j), z, core) for j in (2, 1, 3)]
    line_y = [device(*plane(i, 0), z, core) for i in (2, 1, 3)]
    signal(barrier, line_x + line_y + [along(1), along(31), other])
    pltpu.make_async_copy(basis, basis_in, local_sem.at[4]).start()
    for n, start in enumerate((theirs, own)):
        for base in (0, HALF):
            here = rows(base + start, OWN)
            pltpu.make_async_copy(grads.at[0, here], g_in.at[here], local_sem.at[n]).start()
            pltpu.make_async_copy(errors.at[0, here], e_in.at[here], local_sem.at[n]).start()

    wait(basis_in, local_sem.at[4])
    blocks[...] = twice(basis_in[...].astype(BF16))
    lanes = lax.broadcasted_iota(jnp.int32, (RANK, 128), 1)
    at = lax.broadcasted_iota(jnp.int32, (RANK, 128), 0)

    def product(start):
        both = []
        for base in (0, HALF):
            here = rows(base + start, CHUNK)
            both.append((g_in[here, :].astype(F32) + e_in[here, :].astype(F32)).astype(BF16))
        value = jnp.concatenate(both, axis=1)
        comb[rows(start, CHUNK), :] = value
        part[rows(start, CHUNK), :] = lax.dot_general(
            value, blocks[...], (((1,), (1,)), ((), ())), preferred_element_type=F32
        )

    order = [((y + i) & 3) * CHUNK for i in range(4)]
    wait(g_in, local_sem.at[0])
    for i in range(4):
        product(theirs + order[i])
    pl.semaphore_wait(barrier, 9)
    signal(tokens.at[0], line_x)
    signal(tokens.at[1], [along(1), along(31)])
    for i in range(4):
        send(part.at[rows(theirs + order[i], CHUNK)], from_core.at[i], core_send.at[i], core_recv.at[i], other)
    wait(g_in, local_sem.at[1])
    for i in range(4):
        product(own + order[i])
    for i in range(4):
        wait(from_core.at[i], core_recv.at[i])
        here = rows(own + order[i], CHUNK)
        part[here, :] = part[here, :] + from_core[i]
        for j in range(4):
            if (i, j) != (0, 0):
                px, py = plane(i, j)
                src = part.at[rows(own + (py * 4 + px) * BLOCK, BLOCK)]
                send(src, plane_in.at[mine], send_sem.at[0], recv_sem.at[0], device(px, py, z, core))
        if i == 0:
            pl.semaphore_wait(tokens.at[0], 3)
            pl.semaphore_wait(tokens.at[1], 2)
            signal(tokens.at[2], [along(2), along(30)])
    plane_in[mine] = part[rows(own + mine * BLOCK, BLOCK), :]
    pl.semaphore_wait(tokens.at[2], 2)
    signal(tokens.at[3], [along(4), along(28)])
    wait(plane_in.at[0:15], recv_sem.at[0])
    total = plane_in[0]
    for n in range(1, 16):
        total = total + plane_in[n]
    plane_sum[...] = total

    for o in (2, 1, 3):
        send(plane_sum.at[rows(near_at(o) * PART, PART)], near_in.at[near], send_sem.at[1], recv_sem.at[1], near_device(o))
    for n, (c, i) in enumerate(mate_offsets):
        index, to = mate(c, i)
        send(comb.at[rows(index * CHUNK, CHUNK)], mates.at[n], send_sem.at[2], recv_sem.at[2], to)
    near_in[near] = plane_sum[rows(near * PART, PART), :]
    wait(near_in.at[0:3], recv_sem.at[1])
    near_sum[...] = ((near_in[0] + near_in[1]) + near_in[2]) + near_in[3]

    pl.semaphore_wait(tokens.at[3], 2)
    for n, o in enumerate(ring_offsets):
        send(near_sum, far_in.at[far], far_send.at[n], far_recv.at[n], in_ring(o))
    far_in[far] = near_sum[...]
    above, below = far_in.at[(far + 2) & 7], far_in.at[(far - 2) & 7]
    wait(near_sum, far_recv.at[1])
    send(above, above, far_send.at[4], far_recv.at[4], in_ring(-2))
    send(above, above, far_send.at[5], far_recv.at[5], in_ring(-1))
    wait(near_sum, far_recv.at[0])
    send(below, below, far_send.at[6], far_recv.at[6], in_ring(1))
    slab = own + y * CHUNK
    wait(mates.at[0:7], recv_sem.at[2])
    for i in range(4):
        here = pl.ds(i * 64, 64)
        total = comb[rows(slab + i * 64, 64), :].astype(F32)
        for n in range(7):
            total = total + mates[n, here, :].astype(F32)
        mate_sum[here, 0 : 2 * COLS], mate_sum[here, 2 * COLS :] = split(total)
    for n in (2, 3, 5, 6, 4):
        wait(near_sum, far_recv.at[n])
    total = far_in[0]
    for n in range(1, 8):
        total = total + far_in[n]
    piece = full.at[rows(slab + x * BLOCK + near * PART, PART)]
    piece[...] = total * (1.0 / replicas)
    for o in (2, 1, 3, 0):
        for j in (2, 1, 3, 0):
            if (o, j) != (0, 0):
                send(piece, piece, send_sem.at[3], recv_sem.at[3], near_device(o, j))
    wait(full.at[0 : 15 * PART], recv_sem.at[3])

    value = jnp.concatenate(split(full[rows(slab, CHUNK), :]), axis=1)
    total = lax.dot_general(value, mate_sum[...], (((0,), (0,)), ((), ())), preferred_element_type=F32)
    total = total[:, 0 : 2 * COLS] + total[:, 2 * COLS :]
    right[...] = (total[0:64, 0:COLS] + total[128:192, 0:COLS]) + (total[64:128, COLS:] + total[192:256, COLS:])
    me, lot = core * 4 + y, rows((core * 4 + y) * 8, 8)
    for o in (2, 1, 3, 0):
        for c, i in mate_offsets + [(0, 0)]:
            if (o, c, i) != (0, 0, 0):
                to_core, to_y = core ^ c, (y + i) & 3
                to = device(x, to_y, (z & 28) | near_at(o), to_core)
                src = right.at[rows((to_core * 4 + to_y) * 8, 8)]
                send(src, right_in.at[near * 8 + me], send_sem.at[4], recv_sem.at[4], to)
    right_in[near * 8 + me] = right[lot, :]
    piece = full.at[rows(slab, CHUNK)]
    for i in (2, 1, 3):
        send(piece, piece, send_sem.at[5], recv_sem.at[5], device(x, (y + i) & 3, z, core))

    def gram_of(start):
        total = None
        for i in range(4):
            here = rows(start + i * CHUNK, CHUNK)
            value = jnp.concatenate(split(full[here, :]), axis=1)
            pieces[here, :] = value
            term = lax.dot_general(value, value, (((0,), (0,)), ((), ())), preferred_element_type=F32)
            total = term if total is None else total + term
        return total

    wait(full.at[0 : 3 * CHUNK], recv_sem.at[5])
    half = full.at[rows(own, OWN)]
    send(half, half, core_send.at[4], core_recv.at[4], other)
    grams[core] = gram_of(own)
    wait(right_in.at[0:31], recv_sem.at[4])
    total = right_in[0]
    for n in range(1, 32):
        total = total + right_in[n]
    right_sum[...] = total
    line = far & 3
    for o in (2, 1, 3):
        send(right_sum, right_far.at[line], send_sem.at[7], recv_sem.at[7], in_line(o))
    right_far[line] = right_sum[...]
    comb_copy = pltpu.make_async_copy(comb, comb_out, local_sem.at[2])
    comb_copy.start()
    wait(half, core_recv.at[4])
    grams[1 - core] = gram_of(theirs)
    gram = grams[0] + grams[1]
    gram = (gram[0:128, 0:128] + gram[128:256, 128:256]) + (gram[0:128, 128:256] + gram[128:256, 0:128])
    gram = gram[0:RANK, :] + pltpu.roll(gram[RANK:128, :], RANK, 1)
    factor = inverse_factor(jnp.where(lanes < RANK, gram, jnp.where(lanes == at + RANK, 1.0, 0.0)))
    inverse = jnp.where(lanes < RANK, 0.0, factor)
    left_inverse = pltpu.roll(inverse, RANK, 1)

    wait(right_far.at[0:3], recv_sem.at[7])
    total = ((right_far[0] + right_far[1]) + right_far[2]) + right_far[3]
    piece = right_full.at[lot]
    piece[...] = total * (1.0 / replicas)
    for c, i in mate_offsets:
        send(piece, piece, send_sem.at[8], recv_sem.at[8], mate(c, i)[1])

    high, low = split(jnp.concatenate([left_inverse, inverse], axis=0))
    weights = jnp.concatenate([jnp.concatenate([high, high], axis=1), jnp.concatenate([low, low], axis=1)], axis=0)
    for i in range(HALF // CHUNK):
        here = pl.ds(i * CHUNK, CHUNK)
        value = lax.dot_general(pieces[here, :], weights, (((1,), (1,)), ((), ())), preferred_element_type=F32)
        q[here, :] = (value[:, 0:128] + value[:, 128:256]).astype(BF16)
    q_copy = pltpu.make_async_copy(q, q_out, local_sem.at[3])
    q_copy.start()
    wait(right_full.at[0:56], recv_sem.at[8])
    right_out[...] = jnp.dot(
        left_inverse[:, 0:RANK], right_full[...], precision=lax.Precision.HIGHEST, preferred_element_type=F32
    )

    for i in range(4):
        wait(from_core.at[i], core_send.at[i])
    wait(half, core_send.at[4])
    wait(plane_in.at[0:15], send_sem.at[0])
    wait(near_in.at[0:3], send_sem.at[1])
    wait(mates.at[0:7], send_sem.at[2])
    wait(full.at[0 : 15 * PART], send_sem.at[3])
    wait(right_in.at[0:31], send_sem.at[4])
    wait(full.at[0 : 3 * CHUNK], send_sem.at[5])
    wait(right_far.at[0:3], send_sem.at[7])
    wait(right_in.at[0:7], send_sem.at[8])
    for n in range(7):
        wait(near_sum, far_send.at[n])
    comb_copy.wait()
    q_copy.wait()


def finish_kernel(q, comb, right, approx, new_errors, new_basis, approx_out, errors_out, sem, basis_sem):
    weights = twice(right[...].astype(BF16))
    copies = [pltpu.make_async_copy(right, new_basis, basis_sem)]
    copies[0].start()
    for i in range(HALF // 512):
        here = pl.ds(i * 512, 512)
        full = jnp.dot(q[here, :], weights, preferred_element_type=F32)
        error = (comb[here, :].astype(F32) - full).astype(BF16)
        full = full.astype(BF16)
        for n in range(2):
            approx_out[n, here, :] = full[:, COLS * n : COLS * (n + 1)]
            errors_out[n, here, :] = error[:, COLS * n : COLS * (n + 1)]
        for n, (src, dst) in enumerate(((approx_out, approx), (errors_out, new_errors))):
            copies.append(pltpu.make_async_copy(src.at[:, here], dst.at[:, here], sem.at[n, i]))
            copies[-1].start()
    for copy in copies:
        copy.wait()


def local(replicas, grads, errors, basis):
    vmem, dma = pltpu.VMEM, pltpu.SemaphoreType.DMA
    anywhere, inside = pl.BlockSpec(memory_space=pl.ANY), pl.BlockSpec(memory_space=vmem)
    q, comb, right = pl.pallas_call(
        functools.partial(exchange_kernel, replicas),
        name="exchange",
        out_shape=(
            jax.ShapeDtypeStruct((HALF, 128), BF16),
            jax.ShapeDtypeStruct((HALF, 2 * COLS), BF16),
            jax.ShapeDtypeStruct((RANK, COLS), F32),
        ),
        in_specs=[pl.BlockSpec(memory_space=pltpu.HBM)] * 3,
        out_specs=(anywhere, anywhere, inside),
        scratch_shapes=[
            vmem((2 * HALF, COLS), BF16), vmem((2 * HALF, COLS), BF16), vmem((RANK, COLS), F32), vmem((HALF, 2 * COLS), BF16),
            vmem((128, 2 * COLS), BF16), vmem((HALF, 128), F32), vmem((4, CHUNK, 128), F32),
            vmem((16, BLOCK, 128), F32), vmem((BLOCK, 128), F32), vmem((4, PART, 128), F32), vmem((PART, 128), F32),
            vmem((8, PART, 128), F32), vmem((HALF, 128), F32), vmem((7, CHUNK, 2 * COLS), BF16),
            vmem((CHUNK, 4 * COLS), BF16),
            vmem((HALF, 256), BF16), vmem((2, 256, 256), F32), vmem((HALF, 128), BF16),
            vmem((RANK, COLS), F32), vmem((32, 8, COLS), F32), vmem((8, COLS), F32),
            vmem((4, 8, COLS), F32), vmem((RANK, COLS), F32),
            dma((5,)), dma((5,)), dma((5,)), dma((9,)), dma((9,)), dma((7,)), dma((7,)),
            pltpu.SemaphoreType.REGULAR((4,)),
        ],
        compiler_params=pltpu.CompilerParams(collective_id=0, has_side_effects=True, vmem_limit_bytes=52 << 20),
    )(grads, errors, pltpu.with_memory_space_constraint(basis.T, pltpu.HBM))
    approx, new_errors, new_basis = pl.pallas_call(
        finish_kernel,
        name="finish",
        out_shape=(jax.ShapeDtypeStruct((2, HALF, COLS), BF16),) * 2 + (jax.ShapeDtypeStruct((RANK, COLS), F32),),
        in_specs=[inside] * 3,
        out_specs=(anywhere,) * 3,
        scratch_shapes=[vmem((2, HALF, COLS), BF16), vmem((2, HALF, COLS), BF16), dma((2, 4)), dma],
        compiler_params=pltpu.CompilerParams(vmem_limit_bytes=16 << 20),
    )(q, comb, right)
    return approx.reshape(2 * HALF, COLS), new_errors.reshape(1, 2 * HALF, COLS), new_basis.T


def solution(mesh):
    placed = (P("dp", None, "tensor"), P("dp", None, "tensor"), P("tensor", None))
    return jax.shard_map(
        functools.partial(local, mesh.shape["dp"]),
        mesh=mesh,
        in_specs=placed,
        out_specs=(P(None, "tensor"), P("dp", None, "tensor"), P("tensor", None)),
        check_vma=False,
    )
```
